128 devices in a mesh: rows: 64 (over x, z, y), cols: 2 (over core).
Axes of the slice: x: 4, y: 4, z: 4, core: 2. Of those that a mesh axis runs over, the one named last changes fastest.
Arguments:
- blocks: bfloat16 [4096, 7, 128, 128], P('rows'), may hold values from -0.1875 to 0.1875
- col_index: int32 [4096, 7], P('rows'), may hold values from 0 to 4095, as said below
- right_vecs: bfloat16 [64, 4096, 128], P('cols', 'rows'), may hold values from -30 to 30
- left_vecs: bfloat16 [64, 4096, 128], P('cols', 'rows'), may hold values from -30 to 30
- ritz: bfloat16 [64, 64], replicated, may hold values from -0.75 to 0.75
Outputs:
- right_res: float32 [64, 4096, 128], P('cols', 'rows')
- left_res: float32 [64, 4096, 128], P('cols', 'rows')
- right_norms: float32 [64], P('cols')
- left_norms: float32 [64], P('cols')
The draws below stay inside these ranges and needn't reach their ends.
Inputs may be any that keep to these rules, and one draw needn't show every extreme that they name: `col_index`: entry 0 of each block row is the row's own index. Device p of rows holds block rows p * 64 to (p + 1) * 64 - 1. The devices form a grid of 2 x (32) subdomains of the slab, p = i * M + j with M = 32, periodic along j. Columns outside a device's own rows lie only on its three face neighbours: (i, j + 1 mod M), (i, j - 1 mod M) and (1 - i, j). Among the entries of one device's block rows exactly 2 have a column on (i, j + 1 mod M), and 1 to 2 on each of the other two.
All inputs are finite; a program needn't handle non-finite values.
Results may differ from the reference program's by a relative error of at most 0.0006.
Values may be sent and summed in bfloat16 or wider, within the bound.
A program may use at most 128 MiB of HBM per device.

```python
import math
import jax
import jax.numpy as jnp
from jax import lax

BLOCK = 128
SLOTS = 7
VECS = 64
SENDS = 2
BROWS = 64
NBLK = 4096


def draw_col_index(key, part):
    key = jax.random.fold_in(key, 11)
    peers = NBLK // BROWS
    half = peers // 2
    spare = BROWS * (SLOTS - 1)
    key_a, key_b, key_c, key_d = jax.random.split(key, 4)
    device = jnp.arange(peers, dtype=jnp.int32)
    layer = device // half
    place = device % half
    ahead = layer * half + (place + 1) % half
    behind = layer * half + (place + half - 1) % half
    across = (device + half) % peers
    neighbours = jnp.stack([ahead, behind, across], axis=1)
    counts = jax.random.randint(key_a, (peers, 3), 1, SENDS + 1)
    which = jnp.arange(3, dtype=jnp.int32)[None, :]
    counts = jnp.where(which == 0, SENDS, counts)
    picks = jax.random.randint(key_b, (peers, 3, SENDS), 0, BROWS)
    remote = neighbours[:, :, None] * BROWS + picks
    live = jnp.arange(SENDS)[None, None, :] < counts[:, :, None]
    pool = jnp.where(live, remote, -1).reshape(peers, 3 * SENDS)
    local_pick = device[:, None] * BROWS + jax.random.randint(key_c, (peers, spare), 0, BROWS)
    orders = jax.vmap(lambda k: jax.random.permutation(k, spare))(jax.random.split(key_d, peers))
    targets = orders[:, :3 * SENDS].astype(jnp.int32)
    fallback = jnp.take_along_axis(local_pick, targets, axis=1)
    values = jnp.where(pool >= 0, pool, fallback)
    lines = jnp.broadcast_to(device[:, None], targets.shape)
    off = local_pick.at[lines, targets].set(values)
    off = off.reshape(NBLK, SLOTS - 1)
    diagonal = jnp.arange(NBLK, dtype=jnp.int32)[:, None]
    return jnp.concatenate([diagonal, off.astype(jnp.int32)], axis=1)


def vectors(key, rise):
    key_a = jax.random.fold_in(key, 0)
    key_d = jax.random.fold_in(key, 3)
    key_e = jax.random.fold_in(key, 4)
    shape = (VECS, NBLK, BLOCK)
    gauss = jax.random.normal(key_a, shape, jnp.float32)
    values = gauss
    position = jnp.arange(NBLK, dtype=jnp.float32) / NBLK
    row_scale = rise ** position * jnp.exp(jax.random.uniform(key_d, (NBLK,), jnp.float32, -0.5, 0.5))
    col_scale = jnp.exp(jax.random.uniform(key_e, (VECS,), jnp.float32, 0.0, math.log(10.0)))
    values = 0.3 * values * row_scale[None, :, None] * col_scale[:, None, None]
    return jnp.clip(values, -30.0, 30.0).astype(jnp.bfloat16)


def draw_right_vecs(key, part):
    key = jax.random.fold_in(key, 21)
    return vectors(key, 3.0)


def draw_left_vecs(key, part):
    key = jax.random.fold_in(key, 31)
    return vectors(key, 3.0)


def block_scale(key, shape, shards, least, top_value):
    loudness = 1.0
    for dim, parts in shards:
        heights = jax.random.uniform(jax.random.fold_in(jax.random.fold_in(key, 6), dim), (parts,), jnp.float32, least / len(shards), top_value / len(shards))
        loudness = loudness * jnp.repeat(jnp.exp(heights), shape[dim] // parts).reshape((-1,) + (1,) * (len(shape) - 1 - dim))
    return loudness


def noise(key, extent, deviation, bound, cuts=(), kind=jnp.bfloat16):
    entries = jax.random.normal(key, extent, jnp.float32) * deviation
    if len(cuts) > 0:
        entries = block_scale(key, extent, cuts, -0.22, 0.18) * entries
    return jnp.clip(entries, min=-bound, max=bound).astype(kind)


def setup_inputs(seed: int = 0) -> dict:
    key_of = jax.random.split(jax.random.key(seed), 6)
    return {
        "blocks": noise(key_of[0], (NBLK, SLOTS, BLOCK, BLOCK), (SLOTS * BLOCK) ** -0.5, 0.1875, ((0, 64),)),
        "col_index": draw_col_index(jax.random.fold_in(key_of[5], 71), 0),
        "right_vecs": draw_right_vecs(jax.random.fold_in(key_of[5], 71), 0),
        "left_vecs": draw_left_vecs(jax.random.fold_in(key_of[5], 71), 0),
        "ritz": noise(key_of[4], (VECS, VECS), VECS ** -0.5, 0.75),
    }


def reference(blocks, col_index, right_vecs, left_vecs, ritz):
    nblk = blocks.shape[0]
    groups = nblk // BROWS
    grouped_blocks = blocks.reshape(groups, BROWS, SLOTS, BLOCK, BLOCK)
    grouped_cols = col_index.reshape(groups, BROWS, SLOTS)
    grouped_left = left_vecs.reshape(VECS, groups, BROWS, BLOCK).transpose(1, 0, 2, 3)

    def advance(acc, item):
        blk, cols, ychunk = item
        flat = cols.reshape(-1).astype(jnp.int32)
        gathered = right_vecs[:, flat, :].astype(jnp.float32).reshape(VECS, BROWS, SLOTS, BLOCK)
        wide = blk.astype(jnp.float32)
        product = jnp.einsum('krsj,rsij->kri', gathered, wide)
        contrib = jnp.einsum('kra,rsab->krsb', ychunk.astype(jnp.float32), wide)
        acc = acc.at[:, flat, :].add(contrib.reshape(VECS, BROWS * SLOTS, BLOCK))
        return (acc, product)
    start = jnp.zeros((VECS, nblk, BLOCK), jnp.float32)
    transposed, products = lax.scan(advance, start, (grouped_blocks, grouped_cols, grouped_left))
    product = products.transpose(1, 0, 2, 3).reshape(VECS, nblk, BLOCK)
    table = ritz.astype(jnp.float32)
    right_shift = jnp.einsum('krb,kq->qrb', right_vecs.astype(jnp.float32), table)
    left_shift = jnp.einsum('krb,qk->qrb', left_vecs.astype(jnp.float32), table)
    right_res = product - right_shift
    left_res = transposed - left_shift
    right_norms = jnp.sqrt(lax.optimization_barrier(jnp.sum(right_res * right_res, axis=(1, 2))))
    left_norms = jnp.sqrt(lax.optimization_barrier(jnp.sum(left_res * left_res, axis=(1, 2))))
    return (right_res, left_res, right_norms, left_norms)
```

```python
import functools

import jax
import jax.numpy as jnp
from jax import lax
from jax.experimental import pallas as pl
from jax.experimental.pallas import tpu as pltpu
from jax.sharding import PartitionSpec as P

MESH = pl.DeviceIdType.MESH
F32 = jnp.float32
BF16 = jnp.bfloat16
I32 = jnp.int32
SLOTS = 7
CHUNKS = 8
ROW_EXT, ROW_PREV, ROW_LAST, ROW_PICK, ROW_TWO = 0, 8, 16, 17, 24
BACK = (1, 0, 2)


def kernel(
    peers, rows, vecs,
    cols_hbm, blocks_hbm, x_hbm, y_hbm, ritz_hbm,
    right_hbm, left_hbm, norm_ref,
    cols, blk, raw, wide, xt, yt, xo, yo, summed, ritz, shift_r, shift_l,
    tab, tab_s, ask_out, ask_in, ask_s, x_out, x_in, t_out, t_in, back, lastc, lastc_s,
    right, left, acc, parts,
    in_sem, blk_sem, loc_sem, out_sem,
    ask_ss, ask_rs, x_ss, x_rs, t_ss, t_rs, o_ss, o_rs, n_ss, n_rs,
):
    me = lax.axis_index("rows")
    core = lax.axis_index("cols")
    half = peers // 2
    entries = rows * SLOTS
    layer, place = me // half, me % half
    near = (
        layer * half + (place + 1) % half,
        layer * half + (place + half - 1) % half,
        (me + half) % peers,
    )
    other = 1 - core
    side = (me // 16, (me // 4) % 4, me % 4)
    step = (16, 4, 1)

    def partner(stage, turn):
        return me + (lax.rem(side[stage] + turn, 4) - side[stage]) * step[stage]

    ins = [
        pltpu.make_async_copy(cols_hbm, cols, in_sem.at[0]),
        pltpu.make_async_copy(y_hbm, raw.at[0], in_sem.at[1]),
        pltpu.make_async_copy(x_hbm, raw.at[1], in_sem.at[2]),
        pltpu.make_async_copy(ritz_hbm, ritz, in_sem.at[3]),
    ]
    for copy in ins:
        copy.start()
    per_chunk = entries // CHUNKS

    def chunk_copy(c):
        span = pl.ds(c * per_chunk, per_chunk)
        return pltpu.make_async_copy(blocks_hbm.at[span], blk.at[span], blk_sem.at[c])

    def start_chunk(c, _):
        chunk_copy(c).start()
        return 0

    lax.fori_loop(0, CHUNKS, start_chunk, 0)

    barrier = pltpu.get_barrier_semaphore()
    for n in range(3):
        pl.semaphore_signal(barrier, inc=1, device_id=(near[n], core), device_id_type=MESH)
    pl.semaphore_signal(barrier, inc=1, device_id=(me, other), device_id_type=MESH)
    for stage in range(3):
        for turn in range(1, 4):
            pl.semaphore_signal(
                barrier, inc=1, device_id=(partner(stage, turn), core), device_id_type=MESH
            )

    ins[0].wait()
    col = cols[...]
    owner = col >> 6
    local = col & 63
    row_id = lax.broadcasted_iota(I32, (SLOTS, rows), 1)
    slot_id = lax.broadcasted_iota(I32, (SLOTS, rows), 0)
    order = row_id * SLOTS + slot_id

    def all_min(v):
        return jnp.min(jnp.min(v, axis=1, keepdims=True), axis=0, keepdims=True)

    def all_max(v):
        return jnp.max(jnp.max(v, axis=1, keepdims=True), axis=0, keepdims=True)

    ext = local
    for n in range(3):
        here = owner == near[n]
        first = all_min(jnp.where(here, order, entries))
        final = all_max(jnp.where(here, order, 0))
        id_first = all_max(jnp.where(order == first, local, 0))
        id_final = all_max(jnp.where(order == final, local, 0))
        ext = jnp.where(here, rows + 2 * n + (order == final).astype(I32), ext)
        ask_out[n, 0:1, :] = jnp.broadcast_to(id_first, (1, 128))
        ask_out[n, 1:2, :] = jnp.broadcast_to(id_final, (1, 128))
        ask_out[n, 2:8, :] = jnp.zeros((6, 128), I32)
        tab[ROW_PICK + 2 * n: ROW_PICK + 2 * n + 1, :] = jnp.broadcast_to(first, (1, 128))
        tab[ROW_PICK + 2 * n + 1: ROW_PICK + 2 * n + 2, :] = jnp.broadcast_to(final, (1, 128))
        tab[ROW_TWO + n: ROW_TWO + n + 1, :] = jnp.broadcast_to(
            (first != final).astype(I32), (1, 128)
        )
    tab[ROW_EXT: ROW_EXT + SLOTS, :rows] = ext

    pl.semaphore_wait(barrier, 13)
    asks = [
        pltpu.make_async_remote_copy(
            src_ref=ask_out.at[n], dst_ref=ask_in.at[BACK[n]],
            send_sem=ask_ss.at[n], recv_sem=ask_rs.at[BACK[n]],
            device_id=(near[n], core), device_id_type=MESH,
        )
        for n in range(3)
    ]
    for copy in asks:
        copy.start()

    col_t = jnp.transpose(
        jnp.concatenate([col.astype(F32), jnp.full((1, rows), -1.0, F32)], axis=0)
    ).astype(I32)
    src_row = lax.broadcasted_iota(I32, (rows, rows), 0)
    dst_row = lax.broadcasted_iota(I32, (rows, rows), 1)
    before, upto = src_row < dst_row, src_row <= dst_row
    src_order = src_row * SLOTS
    src_col = [jnp.broadcast_to(col_t[:, s:s + 1], (rows, rows)) for s in range(SLOTS)]
    for s in range(SLOTS):
        mine = jnp.broadcast_to(col[s:s + 1, :], (rows, rows))
        best = jnp.full((rows, rows), -1, I32)
        for t in range(SLOTS):
            best = jnp.where(
                (src_col[t] == mine) & (upto if t < s else before), src_order + t, best
            )
        found = jnp.max(best, axis=0, keepdims=True)
        found = jnp.where((found < 0) | (owner[s:s + 1, :] != me), entries, found)
        tab[ROW_PREV + s: ROW_PREV + s + 1, :rows] = found
    best = jnp.full((rows, rows), 0, I32)
    for t in range(SLOTS):
        best = jnp.where(src_col[t] == dst_row + me * rows, src_order + t, best)
    tab[ROW_LAST: ROW_LAST + 1, :rows] = jnp.max(best, axis=0, keepdims=True)
    tab_copy = pltpu.make_async_copy(tab, tab_s, loc_sem.at[0])
    tab_copy.start()

    def by_rows(index, dst):
        def widen(k, _):
            wide[pl.ds(k * rows, rows), :] = raw[index, k].astype(F32)
            return 0

        lax.fori_loop(0, vecs, widen, 0, unroll=4)

        def turn(r, _):
            dst[r] = wide[pl.ds(r, vecs, stride=rows), :].astype(BF16)
            return 0

        lax.fori_loop(0, rows, turn, 0, unroll=8)

    def across(src, dst, slot):
        return pltpu.make_async_remote_copy(
            src_ref=src, dst_ref=dst, send_sem=o_ss.at[slot], recv_sem=o_rs.at[slot],
            device_id=(me, other), device_id_type=MESH,
        )

    ins[1].wait()
    by_rows(0, yt)
    y_send = across(yt, yo, 0)
    y_send.start()
    ins[2].wait()
    by_rows(1, xt)
    x_send = across(xt.at[pl.ds(0, rows)], xo, 1)
    x_send.start()

    ins[3].wait()
    table = ritz[...].astype(F32)
    low = core == 0
    picked = jnp.where(low, table[:, :vecs], table[:, vecs:])
    picked = jnp.concatenate(
        [jnp.where(low, picked[:vecs], picked[vecs:]), jnp.where(low, picked[vecs:], picked[:vecs])],
        axis=0,
    )
    shift_r[...] = (-jnp.transpose(picked)).astype(BF16)
    picked = jnp.where(low, table[:vecs], table[vecs:])
    picked = jnp.concatenate(
        [
            jnp.where(low, picked[:, :vecs], picked[:, vecs:]),
            jnp.where(low, picked[:, vecs:], picked[:, :vecs]),
        ],
        axis=1,
    )
    shift_l[...] = (-picked).astype(BF16)
    summed[entries] = jnp.zeros((vecs, 128), F32)
    tab_copy.wait()

    x_backs = [
        pltpu.make_async_remote_copy(
            src_ref=x_out.at[n], dst_ref=x_in.at[BACK[n]],
            send_sem=x_ss.at[n], recv_sem=x_rs.at[BACK[n]],
            device_id=(near[n], core), device_id_type=MESH,
        )
        for n in range(3)
    ]

    rows_per = rows // CHUNKS

    def left_chunk(c, _):
        chunk_copy(c).wait()

        def left_row(i, _):
            r = c * rows_per + i
            use = [blk[r * SLOTS + s] for s in range(SLOTS)]
            prod = jnp.dot(yt[r], jnp.concatenate(use, axis=1), preferred_element_type=F32)
            for s in range(SLOTS):
                e = r * SLOTS + s
                summed[e] = prod[:, s * 128:(s + 1) * 128] + summed[tab_s[ROW_PREV + s, r]]
                blk[e] = use[s].T
            return 0

        lax.fori_loop(0, rows_per, left_row, 0, unroll=rows_per)

        @pl.when(c == CHUNKS // 2)
        def _():
            for n in range(3):
                asks[n].wait()
            copy = pltpu.make_async_copy(ask_in, ask_s, loc_sem.at[1])
            copy.start()
            copy.wait()
            for n in range(3):
                for t in range(2):
                    x_out[n, t] = xt[ask_s[n, t, 0]]
                x_backs[n].start()

        return 0

    lax.fori_loop(0, CHUNKS, left_chunk, 0)

    t_sends = []
    for n in range(3):
        two = jnp.broadcast_to(tab[ROW_TWO + n: ROW_TWO + n + 1, :], (vecs, 128)) > 0
        t_out[n, 0] = summed[tab_s[ROW_PICK + 2 * n, 0]].astype(BF16)
        t_out[n, 1] = jnp.where(two, summed[tab_s[ROW_PICK + 2 * n + 1, 0]], 0.0).astype(BF16)
        copy = pltpu.make_async_remote_copy(
            src_ref=t_out.at[n], dst_ref=t_in.at[BACK[n]],
            send_sem=t_ss.at[n], recv_sem=t_rs.at[BACK[n]],
            device_id=(near[n], core), device_id_type=MESH,
        )
        copy.start()
        t_sends.append(copy)

    lane = lax.broadcasted_iota(I32, (1, 128), 1)
    latest = jnp.full((1, 128), 6, I32)
    for u in range(6):
        latest = jnp.where(ask_in[u // 2, u % 2: u % 2 + 1, :] == lane, u, latest)
    lastc[0:1, :] = latest
    lastc_copy = pltpu.make_async_copy(lastc, lastc_s, loc_sem.at[2])
    lastc_copy.start()

    x_send.wait()
    for n in range(3):
        x_backs[n].wait()
    for n in range(3):
        for t in range(2):
            xt[rows + 2 * n + t] = x_in[n, t]

    def right_row(r, total):
        lhs = [xt[tab_s[ROW_EXT + s, r]] for s in range(SLOTS)] + [shift_r[...]]
        rhs = [blk[r * SLOTS + s] for s in range(SLOTS)] + [xt[r], xo[r]]
        res = jnp.dot(
            jnp.concatenate(lhs, axis=1), jnp.concatenate(rhs, axis=0), preferred_element_type=F32
        )
        right[pl.ds(r, vecs, stride=rows), :] = res
        return total + res * res

    acc[0:vecs] = lax.fori_loop(0, rows, right_row, jnp.zeros((vecs, 128), F32), unroll=8)
    right_out = pltpu.make_async_copy(right, right_hbm, out_sem.at[0])
    right_out.start()

    lastc_copy.wait()
    y_send.wait()
    back[6] = jnp.zeros((vecs, 128), F32)
    for n in range(3):
        t_sends[n].wait()
    for u in range(6):
        prev = jnp.int32(6)
        for v in range(u):
            prev = jnp.where(
                ask_s[v // 2, v % 2, 0] == ask_s[u // 2, u % 2, 0], jnp.int32(v), prev
            )
        back[u] = t_in[u // 2, u % 2].astype(F32) + back[prev]

    def left_res(c, total):
        rhs = jnp.concatenate([yt[c], yo[c]], axis=0)
        res = jnp.dot(shift_l[...], rhs, preferred_element_type=F32)
        res = res + summed[tab_s[ROW_LAST, c]] + back[lastc_s[0, c]]
        left[pl.ds(c, vecs, stride=rows), :] = res
        return total + res * res

    acc[vecs: 2 * vecs] = lax.fori_loop(0, rows, left_res, jnp.zeros((vecs, 128), F32), unroll=8)
    left_out = pltpu.make_async_copy(left, left_hbm, out_sem.at[1])
    left_out.start()

    mine = jnp.sum(jnp.transpose(acc[...]), axis=0, keepdims=True)
    mine = jnp.concatenate([mine, jnp.zeros((1, 128 - 2 * vecs), F32)], axis=1)
    for stage in range(3):
        parts[stage, side[stage]] = mine
        sends = []
        for turn in range(1, 4):
            copy = pltpu.make_async_remote_copy(
                src_ref=parts.at[stage, side[stage]],
                dst_ref=parts.at[stage, side[stage]],
                send_sem=n_ss.at[stage, turn], recv_sem=n_rs.at[stage, side[stage]],
                device_id=(partner(stage, turn), core), device_id_type=MESH,
            )
            copy.start()
            sends.append(copy)
        for turn in range(1, 4):
            sender = lax.rem(side[stage] + turn, 4)
            pltpu.make_async_remote_copy(
                src_ref=parts.at[stage, sender], dst_ref=parts.at[stage, sender],
                send_sem=n_ss.at[stage, turn], recv_sem=n_rs.at[stage, sender],
                device_id=(partner(stage, turn), core), device_id_type=MESH,
            ).wait_recv()
        for copy in sends:
            copy.wait_send()
        mine = parts[stage, 0] + parts[stage, 1] + parts[stage, 2] + parts[stage, 3]
    norm_ref[...] = mine
    right_out.wait()
    left_out.wait()


def shards(blocks, col_index, right_vecs, left_vecs, ritz):
    peers = lax.axis_size("rows")
    rows, slots = col_index.shape
    vecs, _, width = right_vecs.shape
    entries = rows * slots
    any_spec = pl.BlockSpec(memory_space=pl.ANY)
    dma = pltpu.SemaphoreType.DMA
    right, left, norms = pl.pallas_call(
        functools.partial(kernel, peers, rows, vecs),
        out_shape=(
            jax.ShapeDtypeStruct((vecs * rows, width), F32),
            jax.ShapeDtypeStruct((vecs * rows, width), F32),
            jax.ShapeDtypeStruct((1, 128), F32),
        ),
        in_specs=[any_spec] * 5,
        out_specs=(any_spec, any_spec, pl.BlockSpec(memory_space=pltpu.VMEM)),
        scratch_shapes=[
            pltpu.VMEM((slots, rows), I32),
            pltpu.VMEM((entries, width, width), BF16),
            pltpu.VMEM((2, vecs, rows, width), BF16),
            pltpu.VMEM((vecs * rows, width), F32),
            pltpu.VMEM((rows + 6, vecs, width), BF16),
            pltpu.VMEM((rows, vecs, width), BF16),
            pltpu.VMEM((rows, vecs, width), BF16),
            pltpu.VMEM((rows, vecs, width), BF16),
            pltpu.VMEM((entries + 1, vecs, width), F32),
            pltpu.VMEM((2 * vecs, 2 * vecs), BF16),
            pltpu.VMEM((vecs, 2 * vecs), BF16),
            pltpu.VMEM((vecs, 2 * vecs), BF16),
            pltpu.VMEM((32, 128), I32),
            pltpu.SMEM((32, 128), I32),
            pltpu.VMEM((3, 8, 128), I32),
            pltpu.VMEM((3, 8, 128), I32),
            pltpu.SMEM((3, 8, 128), I32),
            pltpu.VMEM((3, 2, vecs, width), BF16),
            pltpu.VMEM((3, 2, vecs, width), BF16),
            pltpu.VMEM((3, 2, vecs, width), BF16),
            pltpu.VMEM((3, 2, vecs, width), BF16),
            pltpu.VMEM((7, vecs, width), F32),
            pltpu.VMEM((8, 128), I32),
            pltpu.SMEM((8, 128), I32),
            pltpu.VMEM((vecs * rows, width), F32),
            pltpu.VMEM((vecs * rows, width), F32),
            pltpu.VMEM((2 * vecs, width), F32),
            pltpu.VMEM((3, 4, 1, 128), F32),
            dma((4,)),
            dma((CHUNKS,)),
            dma((3,)),
            dma((2,)),
            dma((3,)), dma((3,)),
            dma((3,)), dma((3,)),
            dma((3,)), dma((3,)),
            dma((2,)), dma((2,)),
            dma((3, 4)), dma((3, 4)),
        ],
        compiler_params=pltpu.CompilerParams(
            collective_id=0, has_side_effects=True, vmem_limit_bytes=48 << 20
        ),
    )(
        col_index.T,
        blocks.reshape(entries, width, width),
        right_vecs,
        left_vecs,
        ritz,
    )
    norms = jnp.sqrt(norms[0, : 2 * vecs])
    return (
        right.reshape(vecs, rows, width),
        left.reshape(vecs, rows, width),
        norms[:vecs],
        norms[vecs:],
    )


def solution(mesh):
    placed = (
        P("rows", None, None, None),
        P("rows", None),
        P("cols", "rows", None),
        P("cols", "rows", None),
        P(),
    )
    return jax.shard_map(
        shards,
        mesh=mesh,
        in_specs=placed,
        out_specs=(P("cols", "rows", None), P("cols", "rows", None), P("cols"), P("cols")),
        check_vma=False,
    )
```

```python
import functools

import jax
import jax.numpy as jnp
from jax import lax
from jax.experimental import pallas as pl
from jax.experimental.pallas import tpu as pltpu
from jax.sharding import PartitionSpec as P

MESH = pl.DeviceIdType.MESH
F32 = jnp.float32
BF16 = jnp.bfloat16
I32 = jnp.int32
SLOTS = 7
CHUNKS = 8
PASSES = 4
OFFSETS = sorted(
    ((a, b, c) for a in range(4) for b in range(4) for c in range(4) if a + b + c),
    key=lambda d: -sum(min(v, 4 - v) for v in d),
)
ROW_EXT, ROW_PREV, ROW_LAST, ROW_PICK, ROW_TWO, ROW_SAME, ROW_FIX = 0, 8, 16, 17, 24, 32, 38
BACK = (1, 0, 2)


def kernel(
    peers, rows, vecs,
    cols_hbm, blocks_hbm, x_hbm, y_hbm, ritz_hbm,
    right_hbm, left_hbm, norm_ref,
    cols, blk, raw, wide, xt, yt, xo, yo, summed, ritz, shift_r, shift_l,
    tab, tab_s, ask_out, ask_in, ask_s, x_out, x_in, t_out, t_in, back, fixes, lastc, lastc_s,
    kept, right, left, acc, parts,
    in_sem, blk_sem, loc_sem, out_sem,
    ask_ss, ask_rs, x_ss, x_rs, t_ss, t_rs, o_ss, o_rs, n_ss, n_rs,
):
    me = lax.axis_index("rows")
    core = lax.axis_index("cols")
    half = peers // 2
    entries = rows * SLOTS
    layer, place = me // half, me % half
    near = (
        layer * half + (place + 1) % half,
        layer * half + (place + half - 1) % half,
        (me + half) % peers,
    )
    other = 1 - core
    side = (me // 16, (me // 4) % 4, me % 4)

    def peer(offset):
        at = [lax.rem(a + d, 4) for a, d in zip(side, offset)]
        return at[0] * 16 + at[1] * 4 + at[2]

    ins = [
        pltpu.make_async_copy(cols_hbm, cols, in_sem.at[0]),
        pltpu.make_async_copy(y_hbm, raw.at[0], in_sem.at[1]),
        pltpu.make_async_copy(x_hbm, raw.at[1], in_sem.at[2]),
        pltpu.make_async_copy(ritz_hbm, ritz, in_sem.at[3]),
    ]
    for copy in ins:
        copy.start()
    per_chunk = entries // CHUNKS

    def chunk_copy(c):
        span = pl.ds(c * per_chunk, per_chunk)
        return pltpu.make_async_copy(blocks_hbm.at[span], blk.at[span], blk_sem.at[c])

    def start_chunk(c, _):
        chunk_copy(c).start()
        return 0

    lax.fori_loop(0, CHUNKS, start_chunk, 0)

    barrier = pltpu.get_barrier_semaphore()
    pl.semaphore_signal(barrier, inc=1, device_id=(me, other), device_id_type=MESH)
    for offset in OFFSETS:
        pl.semaphore_signal(barrier, inc=1, device_id=(peer(offset), core), device_id_type=MESH)

    ins[0].wait()
    col = cols[...]
    owner = col >> 6
    local = col & 63
    row_id = lax.broadcasted_iota(I32, (SLOTS, rows), 1)
    slot_id = lax.broadcasted_iota(I32, (SLOTS, rows), 0)
    order = row_id * SLOTS + slot_id

    def all_min(v):
        return jnp.min(jnp.min(v, axis=1, keepdims=True), axis=0, keepdims=True)

    def all_max(v):
        return jnp.max(jnp.max(v, axis=1, keepdims=True), axis=0, keepdims=True)

    def put(row, value):
        tab[row: row + 1, :] = jnp.broadcast_to(value, (1, 128))

    lane = lax.broadcasted_iota(I32, (1, 128), 1)
    tab[ROW_EXT: ROW_EXT + SLOTS, :rows] = jnp.where(owner == me, local, rows)
    fix = jnp.full((1, 128), 6, I32)
    pick_rows = []
    for n in range(3):
        here = owner == near[n]
        first = all_min(jnp.where(here, order, entries))
        final = all_max(jnp.where(here, order, 0))
        picks = (first, final)
        for t in range(2):
            hit = order == picks[t]
            ask_out[n, t: t + 1, :] = jnp.broadcast_to(
                all_max(jnp.where(hit, local, 0)), (1, 128)
            )
            put(ROW_PICK + 2 * n + t, jnp.minimum(picks[t], entries - 1))
            at = all_max(jnp.where(hit, row_id, 0))
            if t == 1:
                at = jnp.where(first == final, -1, at)
            same = jnp.full((1, 1), 6, I32)
            for v, earlier in enumerate(pick_rows):
                same = jnp.where(earlier == at, v, same)
            put(ROW_SAME + 2 * n + t, same)
            fix = jnp.where(lane == at, 2 * n + t, fix)
            pick_rows.append(at)
        ask_out[n, 2:8, :] = jnp.zeros((6, 128), I32)
        put(ROW_TWO + n, (first != final).astype(I32))
    put(ROW_FIX, fix)

    asks = [
        pltpu.make_async_remote_copy(
            src_ref=ask_out.at[n], dst_ref=ask_in.at[BACK[n]],
            send_sem=ask_ss.at[n], recv_sem=ask_rs.at[BACK[n]],
            device_id=(near[n], core), device_id_type=MESH,
        )
        for n in range(3)
    ]

    col_t = jnp.transpose(
        jnp.concatenate([col.astype(F32), jnp.full((1, rows), -1.0, F32)], axis=0)
    ).astype(I32)
    src_row = lax.broadcasted_iota(I32, (rows, rows), 0)
    dst_row = lax.broadcasted_iota(I32, (rows, rows), 1)
    before, upto = src_row < dst_row, src_row <= dst_row
    src_order = src_row * SLOTS
    src_col = [jnp.broadcast_to(col_t[:, s:s + 1], (rows, rows)) for s in range(SLOTS)]
    for s in range(SLOTS):
        mine = jnp.broadcast_to(col[s:s + 1, :], (rows, rows))
        best = jnp.full((rows, rows), -1, I32)
        for t in range(SLOTS):
            best = jnp.where(
                (src_col[t] == mine) & (upto if t < s else before), src_order + t, best
            )
        found = jnp.max(best, axis=0, keepdims=True)
        found = jnp.where((found < 0) | (owner[s:s + 1, :] != me), entries, found)
        tab[ROW_PREV + s: ROW_PREV + s + 1, :rows] = found
    best = jnp.full((rows, rows), 0, I32)
    for t in range(SLOTS):
        best = jnp.where(src_col[t] == dst_row + me * rows, src_order + t, best)
    tab[ROW_LAST: ROW_LAST + 1, :rows] = jnp.max(best, axis=0, keepdims=True)
    tab_copy = pltpu.make_async_copy(tab, tab_s, loc_sem.at[0])
    tab_copy.start()

    def by_rows(index, dst):
        def widen(k, _):
            wide[pl.ds(k * rows, rows), :] = raw[index, k].astype(F32)
            return 0

        lax.fori_loop(0, vecs, widen, 0, unroll=4)

        def turn(r, _):
            dst[r] = wide[pl.ds(r, vecs, stride=rows), :].astype(BF16)
            return 0

        lax.fori_loop(0, rows, turn, 0, unroll=8)

    def across(src, dst, slot):
        return pltpu.make_async_remote_copy(
            src_ref=src, dst_ref=dst, send_sem=o_ss.at[slot], recv_sem=o_rs.at[slot],
            device_id=(me, other), device_id_type=MESH,
        )

    ins[1].wait()
    by_rows(0, yt)
    y_send = across(yt, yo, 0)
    ins[2].wait()
    by_rows(1, xt)
    x_send = across(xt.at[pl.ds(0, rows)], xo, 1)

    ins[3].wait()
    table = ritz[...].astype(F32)
    low = core == 0
    picked = jnp.where(low, table[:, :vecs], table[:, vecs:])
    picked = jnp.concatenate(
        [jnp.where(low, picked[:vecs], picked[vecs:]), jnp.where(low, picked[vecs:], picked[:vecs])],
        axis=0,
    )
    shift_r[...] = (-jnp.transpose(picked)).astype(BF16)
    picked = jnp.where(low, table[:vecs], table[vecs:])
    picked = jnp.concatenate(
        [
            jnp.where(low, picked[:, :vecs], picked[:, vecs:]),
            jnp.where(low, picked[:, vecs:], picked[:, :vecs]),
        ],
        axis=1,
    )
    shift_l[...] = (-picked).astype(BF16)
    summed[entries] = jnp.zeros((vecs, 128), F32)

    x_backs = [
        pltpu.make_async_remote_copy(
            src_ref=x_out.at[n], dst_ref=x_in.at[BACK[n]],
            send_sem=x_ss.at[n], recv_sem=x_rs.at[BACK[n]],
            device_id=(near[n], core), device_id_type=MESH,
        )
        for n in range(3)
    ]

    xt[rows] = jnp.zeros((vecs, 128), BF16)
    pl.semaphore_wait(barrier, peers)
    for copy in asks:
        copy.start()
    y_send.start()
    x_send.start()
    tab_copy.wait()

    per_pass = rows // PASSES

    ask_copy = pltpu.make_async_copy(ask_in, ask_s, loc_sem.at[1])
    lastc_copy = pltpu.make_async_copy(lastc, lastc_s, loc_sem.at[2])

    def one_pass(c, _):
        for half_pass in range(CHUNKS // PASSES):
            chunk_copy(c * (CHUNKS // PASSES) + half_pass).wait()

        @pl.when(c == 2)
        def _():
            for n in range(3):
                asks[n].wait()
            ask_copy.start()
            latest = jnp.full((1, 128), 6, I32)
            for u in range(6):
                latest = jnp.where(ask_in[u // 2, u % 2: u % 2 + 1, :] == lane, u, latest)
            lastc[0:1, :] = latest
            lastc_copy.start()

        @pl.when(c == 3)
        def _():
            ask_copy.wait()
            lastc_copy.wait()
            for n in range(3):
                for t in range(2):
                    x_out[n, t] = xt[ask_s[n, t, 0]]
                x_backs[n].start()

        def both(i, _):
            r = c * per_pass + i
            use = [blk[r * SLOTS + s] for s in range(SLOTS)]
            prod = jnp.dot(yt[r], jnp.concatenate(use, axis=1), preferred_element_type=F32)
            lhs = [xt[tab_s[ROW_EXT + s, r]] for s in range(SLOTS)]
            kept[r] = jnp.dot(
                jnp.concatenate(lhs, axis=1),
                jnp.concatenate([block.T for block in use], axis=0),
                preferred_element_type=F32,
            )
            for s in range(SLOTS):
                summed[r * SLOTS + s] = (
                    prod[:, s * 128:(s + 1) * 128] + summed[tab_s[ROW_PREV + s, r]]
                )
            return 0

        lax.fori_loop(0, per_pass, both, 0, unroll=True)
        return 0

    lax.fori_loop(0, PASSES, one_pass, 0)

    t_sends = []
    for n in range(3):
        two = jnp.broadcast_to(tab[ROW_TWO + n: ROW_TWO + n + 1, :], (vecs, 128)) > 0
        t_out[n, 0] = summed[tab_s[ROW_PICK + 2 * n, 0]].astype(BF16)
        t_out[n, 1] = jnp.where(two, summed[tab_s[ROW_PICK + 2 * n + 1, 0]], 0.0).astype(BF16)
        copy = pltpu.make_async_remote_copy(
            src_ref=t_out.at[n], dst_ref=t_in.at[BACK[n]],
            send_sem=t_ss.at[n], recv_sem=t_rs.at[BACK[n]],
            device_id=(near[n], core), device_id_type=MESH,
        )
        copy.start()
        t_sends.append(copy)

    for n in range(3):
        x_backs[n].wait()
    fixes[6] = jnp.zeros((vecs, 128), F32)
    for u in range(6):
        fixes[u] = lax.dot_general(
            x_in[u // 2, u % 2], blk[tab_s[ROW_PICK + u, 0]], (((1,), (1,)), ((), ())),
            preferred_element_type=F32,
        ) + fixes[tab_s[ROW_SAME + u, 0]]
    x_send.wait()
    y_send.wait()

    def right_row(r, total):
        res = jnp.dot(
            shift_r[...], jnp.concatenate([xt[r], xo[r]], axis=0), preferred_element_type=F32
        )
        res = res + kept[r] + fixes[tab_s[ROW_FIX, r]]
        right[pl.ds(r, vecs, stride=rows), :] = res
        return total + res * res

    acc[0:vecs] = lax.fori_loop(0, rows, right_row, jnp.zeros((vecs, 128), F32), unroll=8)
    right_out = pltpu.make_async_copy(right, right_hbm, out_sem.at[0])
    right_out.start()

    back[6] = jnp.zeros((vecs, 128), F32)
    for n in range(3):
        t_sends[n].wait()
    for u in range(6):
        prev = jnp.int32(6)
        for v in range(u):
            prev = jnp.where(
                ask_s[v // 2, v % 2, 0] == ask_s[u // 2, u % 2, 0], jnp.int32(v), prev
            )
        back[u] = t_in[u // 2, u % 2].astype(F32) + back[prev]

    def left_res(c, total):
        res = jnp.dot(
            shift_l[...], jnp.concatenate([yt[c], yo[c]], axis=0), preferred_element_type=F32
        )
        res = res + summed[tab_s[ROW_LAST, c]] + back[lastc_s[0, c]]
        left[pl.ds(c, vecs, stride=rows), :] = res
        return total + res * res

    acc[vecs: 2 * vecs] = lax.fori_loop(0, rows, left_res, jnp.zeros((vecs, 128), F32), unroll=8)
    left_out = pltpu.make_async_copy(left, left_hbm, out_sem.at[1])
    left_out.start()

    mine = jnp.sum(jnp.transpose(acc[...]), axis=0, keepdims=True)
    mine = jnp.concatenate([mine, jnp.zeros((1, 128 - 2 * vecs), F32)], axis=1)
    parts[me] = mine

    def share(to):
        return pltpu.make_async_remote_copy(
            src_ref=parts.at[me], dst_ref=parts.at[me], send_sem=n_ss.at[0], recv_sem=n_rs.at[0],
            device_id=(to, core), device_id_type=MESH,
        )

    for offset in OFFSETS:
        share(peer(offset)).start()
    every = pltpu.make_async_remote_copy(
        src_ref=parts.at[pl.ds(0, peers - 1)], dst_ref=parts.at[pl.ds(0, peers - 1)],
        send_sem=n_ss.at[0], recv_sem=n_rs.at[0],
        device_id=(near[0], core), device_id_type=MESH,
    )
    every.wait_recv()
    every.wait_send()
    norm_ref[...] = jnp.sqrt(jnp.sum(parts[...], axis=0))
    right_out.wait()
    left_out.wait()


def shards(blocks, col_index, right_vecs, left_vecs, ritz):
    peers = lax.axis_size("rows")
    rows, slots = col_index.shape
    vecs, _, width = right_vecs.shape
    entries = rows * slots
    any_spec = pl.BlockSpec(memory_space=pl.ANY)
    dma = pltpu.SemaphoreType.DMA
    right, left, norms = pl.pallas_call(
        functools.partial(kernel, peers, rows, vecs),
        out_shape=(
            jax.ShapeDtypeStruct((vecs * rows, width), F32),
            jax.ShapeDtypeStruct((vecs * rows, width), F32),
            jax.ShapeDtypeStruct((1, 128), F32),
        ),
        in_specs=[any_spec] * 5,
        out_specs=(any_spec, any_spec, pl.BlockSpec(memory_space=pltpu.VMEM)),
        scratch_shapes=[
            pltpu.VMEM((slots, rows), I32),
            pltpu.VMEM((entries, width, width), BF16),
            pltpu.VMEM((2, vecs, rows, width), BF16),
            pltpu.VMEM((vecs * rows, width), F32),
            pltpu.VMEM((rows + 1, vecs, width), BF16),
            pltpu.VMEM((rows, vecs, width), BF16),
            pltpu.VMEM((rows, vecs, width), BF16),
            pltpu.VMEM((rows, vecs, width), BF16),
            pltpu.VMEM((entries + 1, vecs, width), F32),
            pltpu.VMEM((2 * vecs, 2 * vecs), BF16),
            pltpu.VMEM((vecs, 2 * vecs), BF16),
            pltpu.VMEM((vecs, 2 * vecs), BF16),
            pltpu.VMEM((40, 128), I32),
            pltpu.SMEM((40, 128), I32),
            pltpu.VMEM((3, 8, 128), I32),
            pltpu.VMEM((3, 8, 128), I32),
            pltpu.SMEM((3, 8, 128), I32),
            pltpu.VMEM((3, 2, vecs, width), BF16),
            pltpu.VMEM((3, 2, vecs, width), BF16),
            pltpu.VMEM((3, 2, vecs, width), BF16),
            pltpu.VMEM((3, 2, vecs, width), BF16),
            pltpu.VMEM((7, vecs, width), F32),
            pltpu.VMEM((7, vecs, width), F32),
            pltpu.VMEM((8, 128), I32),
            pltpu.SMEM((8, 128), I32),
            pltpu.VMEM((rows, vecs, width), F32),
            pltpu.VMEM((vecs * rows, width), F32),
            pltpu.VMEM((vecs * rows, width), F32),
            pltpu.VMEM((2 * vecs, width), F32),
            pltpu.VMEM((peers, 1, 128), F32),
            dma((4,)),
            dma((CHUNKS,)),
            dma((3,)),
            dma((2,)),
            dma((3,)), dma((3,)),
            dma((3,)), dma((3,)),
            dma((3,)), dma((3,)),
            dma((2,)), dma((2,)),
            dma((1,)), dma((1,)),
        ],
        compiler_params=pltpu.CompilerParams(
            collective_id=0, has_side_effects=True, vmem_limit_bytes=63 << 20
        ),
    )(
        col_index.T,
        blocks.reshape(entries, width, width),
        right_vecs,
        left_vecs,
        ritz,
    )
    norms = norms[0, : 2 * vecs]
    return (
        right.reshape(vecs, rows, width),
        left.reshape(vecs, rows, width),
        norms[:vecs],
        norms[vecs:],
    )


def solution(mesh):
    placed = (
        P("rows", None, None, None),
        P("rows", None),
        P("cols", "rows", None),
        P("cols", "rows", None),
        P(),
    )
    return jax.shard_map(
        shards,
        mesh=mesh,
        in_specs=placed,
        out_specs=(P("cols", "rows", None), P("cols", "rows", None), P("cols"), P("cols")),
        check_vma=False,
    )
```

```python
import functools

import jax
import jax.numpy as jnp
from jax import lax
from jax.experimental import pallas as pl
from jax.experimental.pallas import tpu as pltpu
from jax.sharding import PartitionSpec as P

MESH = pl.DeviceIdType.MESH
F32 = jnp.float32
BF16 = jnp.bfloat16
I32 = jnp.int32
SLOTS = 7
CHUNKS = 8
PASSES = 4
OFFSETS = sorted(
    ((a, b, c) for a in range(4) for b in range(4) for c in range(4) if a + b + c),
    key=lambda d: -sum(min(v, 4 - v) for v in d),
)
ROW_EXT, ROW_PREV, ROW_LAST, ROW_PICK, ROW_TWO, ROW_SAME, ROW_FIX, ROW_AT = 0, 8, 16, 17, 24, 32, 38, 40
BACK = (1, 0, 2)


def kernel(
    peers, rows, vecs,
    cols_hbm, blocks_hbm, x_hbm, y_hbm, ritz_hbm,
    right_hbm, left_hbm, norm_ref,
    cols, blk, raw, wide, xt, yt, xo, yo, summed, ritz, shift_r, shift_l,
    tab, tab_s, ask_out, ask_in, ask_s, x_out, x_in, t_out, t_in, back, fixes, lastc, lastc_s,
    kept, kept_l, acc, parts,
    in_sem, blk_sem, loc_sem, out_sem,
    ask_ss, ask_rs, x_ss, x_rs, t_ss, t_rs, o_ss, o_rs, n_ss, n_rs, all_x, all_z,
):
    me = lax.axis_index("rows")
    core = lax.axis_index("cols")
    half = peers // 2
    entries = rows * SLOTS
    layer, place = me // half, me % half
    near = (
        layer * half + (place + 1) % half,
        layer * half + (place + half - 1) % half,
        (me + half) % peers,
    )
    other = 1 - core
    side = (me // 16, (me // 4) % 4, me % 4)

    def peer(offset):
        at = [lax.rem(a + d, 4) for a, d in zip(side, offset)]
        return at[0] * 16 + at[1] * 4 + at[2]

    ins = [
        pltpu.make_async_copy(cols_hbm, cols, in_sem.at[0]),
        pltpu.make_async_copy(y_hbm, raw.at[0], in_sem.at[1]),
        pltpu.make_async_copy(x_hbm, raw.at[1], in_sem.at[2]),
        pltpu.make_async_copy(ritz_hbm, ritz, in_sem.at[3]),
    ]
    for copy in ins:
        copy.start()
    per_chunk = entries // CHUNKS

    def chunk_copy(c):
        span = pl.ds(c * per_chunk, per_chunk)
        return pltpu.make_async_copy(blocks_hbm.at[span], blk.at[span], blk_sem.at[c])

    def start_chunk(c, _):
        chunk_copy(c).start()
        return 0

    lax.fori_loop(0, CHUNKS, start_chunk, 0)

    barrier = pltpu.get_barrier_semaphore()
    lines = [
        [peer(tuple(d if a == axis else 0 for a in range(3))) for d in range(1, 4)]
        for axis in range(3)
    ]
    met = list(near) + lines[0] + lines[1] + lines[2]
    pl.semaphore_signal(barrier, inc=1, device_id=(me, other), device_id_type=MESH)
    for to in met:
        pl.semaphore_signal(barrier, inc=1, device_id=(to, core), device_id_type=MESH)

    ins[0].wait()
    col = cols[...]
    owner = col >> 6
    local = col & 63
    row_id = lax.broadcasted_iota(I32, (SLOTS, rows), 1)
    slot_id = lax.broadcasted_iota(I32, (SLOTS, rows), 0)
    order = row_id * SLOTS + slot_id

    def all_min(v):
        return jnp.min(jnp.min(v, axis=1, keepdims=True), axis=0, keepdims=True)

    def all_max(v):
        return jnp.max(jnp.max(v, axis=1, keepdims=True), axis=0, keepdims=True)

    def put(row, value):
        tab[row: row + 1, :] = jnp.broadcast_to(value, (1, 128))

    lane = lax.broadcasted_iota(I32, (1, 128), 1)
    tab[ROW_EXT: ROW_EXT + SLOTS, :rows] = jnp.where(owner == me, local, rows)
    fix = jnp.full((1, 128), 6, I32)
    pick_rows = []
    for n in range(3):
        here = owner == near[n]
        first = all_min(jnp.where(here, order, entries))
        final = all_max(jnp.where(here, order, 0))
        picks = (first, final)
        for t in range(2):
            hit = order == picks[t]
            ask_out[n, t: t + 1, :] = jnp.broadcast_to(
                all_max(jnp.where(hit, local, 0)), (1, 128)
            )
            put(ROW_PICK + 2 * n + t, jnp.minimum(picks[t], entries - 1))
            at = all_max(jnp.where(hit, row_id, 0))
            put(ROW_AT + 2 * n + t, at)
            if t == 1:
                at = jnp.where(first == final, -1, at)
            same = jnp.full((1, 1), 6, I32)
            for v, earlier in enumerate(pick_rows):
                same = jnp.where(earlier == at, v, same)
            put(ROW_SAME + 2 * n + t, same)
            fix = jnp.where(lane == at, 2 * n + t, fix)
            pick_rows.append(at)
        ask_out[n, 2:8, :] = jnp.zeros((6, 128), I32)
        put(ROW_TWO + n, (first != final).astype(I32))
    put(ROW_FIX, fix)

    pl.semaphore_wait(barrier, len(met) + 1)
    asks = [
        pltpu.make_async_remote_copy(
            src_ref=ask_out.at[n], dst_ref=ask_in.at[BACK[n]],
            send_sem=ask_ss.at[n], recv_sem=ask_rs.at[BACK[n]],
            device_id=(near[n], core), device_id_type=MESH,
        )
        for n in range(3)
    ]

    for copy in asks:
        copy.start()
    for to in lines[0]:
        pl.semaphore_signal(all_x, inc=1, device_id=(to, core), device_id_type=MESH)

    col_t = jnp.transpose(
        jnp.concatenate([col.astype(F32), jnp.full((1, rows), -1.0, F32)], axis=0)
    ).astype(I32)
    src_row = lax.broadcasted_iota(I32, (rows, rows), 0)
    dst_row = lax.broadcasted_iota(I32, (rows, rows), 1)
    before, upto = src_row < dst_row, src_row <= dst_row
    src_order = src_row * SLOTS
    src_col = [jnp.broadcast_to(col_t[:, s:s + 1], (rows, rows)) for s in range(SLOTS)]
    for s in range(SLOTS):
        mine = jnp.broadcast_to(col[s:s + 1, :], (rows, rows))
        best = jnp.full((rows, rows), -1, I32)
        for t in range(SLOTS):
            best = jnp.where(
                (src_col[t] == mine) & (upto if t < s else before), src_order + t, best
            )
        found = jnp.max(best, axis=0, keepdims=True)
        found = jnp.where((found < 0) | (owner[s:s + 1, :] != me), entries, found)
        tab[ROW_PREV + s: ROW_PREV + s + 1, :rows] = found
    best = jnp.full((rows, rows), 0, I32)
    for t in range(SLOTS):
        best = jnp.where(src_col[t] == dst_row + me * rows, src_order + t, best)
    tab[ROW_LAST: ROW_LAST + 1, :rows] = jnp.max(best, axis=0, keepdims=True)
    tab_copy = pltpu.make_async_copy(tab, tab_s, loc_sem.at[0])
    tab_copy.start()

    def by_rows(index, dst):
        def widen(k, _):
            wide[pl.ds(k * rows, rows), :] = raw[index, k].astype(F32)
            return 0

        lax.fori_loop(0, vecs, widen, 0, unroll=4)

        def turn(r, _):
            dst[r] = wide[pl.ds(r, vecs, stride=rows), :].astype(BF16)
            return 0

        lax.fori_loop(0, rows, turn, 0, unroll=8)

    def across(src, dst, slot):
        return pltpu.make_async_remote_copy(
            src_ref=src, dst_ref=dst, send_sem=o_ss.at[slot], recv_sem=o_rs.at[slot],
            device_id=(me, other), device_id_type=MESH,
        )

    ins[1].wait()
    by_rows(0, yt)
    y_send = across(yt, yo, 0)
    y_send.start()
    ins[2].wait()
    by_rows(1, xt)
    x_send = across(xt.at[pl.ds(0, rows)], xo, 1)
    x_send.start()

    ins[3].wait()
    table = ritz[...].astype(F32)
    low = core == 0
    picked = jnp.where(low, table[:, :vecs], table[:, vecs:])
    picked = jnp.concatenate(
        [jnp.where(low, picked[:vecs], picked[vecs:]), jnp.where(low, picked[vecs:], picked[:vecs])],
        axis=0,
    )
    shift_r[...] = (-jnp.transpose(picked)).astype(BF16)
    picked = jnp.where(low, table[:vecs], table[vecs:])
    picked = jnp.concatenate(
        [
            jnp.where(low, picked[:, :vecs], picked[:, vecs:]),
            jnp.where(low, picked[:, vecs:], picked[:, :vecs]),
        ],
        axis=1,
    )
    shift_l[...] = (-picked).astype(BF16)
    summed[entries] = jnp.zeros((vecs, 128), F32)

    x_backs = [
        pltpu.make_async_remote_copy(
            src_ref=x_out.at[n], dst_ref=x_in.at[BACK[n]],
            send_sem=x_ss.at[n], recv_sem=x_rs.at[BACK[n]],
            device_id=(near[n], core), device_id_type=MESH,
        )
        for n in range(3)
    ]

    xt[rows] = jnp.zeros((vecs, 128), BF16)
    tab_copy.wait()

    per_pass = rows // PASSES

    ask_copy = pltpu.make_async_copy(ask_in, ask_s, loc_sem.at[1])
    lastc_copy = pltpu.make_async_copy(lastc, lastc_s, loc_sem.at[2])
    t_sends = [
        pltpu.make_async_remote_copy(
            src_ref=t_out.at[n], dst_ref=t_in.at[BACK[n]],
            send_sem=t_ss.at[n], recv_sem=t_rs.at[BACK[n]],
            device_id=(near[n], core), device_id_type=MESH,
        )
        for n in range(3)
    ]

    def one_pass(c, _):
        for half_pass in range(CHUNKS // PASSES):
            chunk_copy(c * (CHUNKS // PASSES) + half_pass).wait()

        @pl.when(c == PASSES - 1)
        def _():
            for n in range(3):
                asks[n].wait()
            ask_copy.start()
            latest = jnp.full((1, 128), 6, I32)
            for u in range(6):
                latest = jnp.where(ask_in[u // 2, u % 2: u % 2 + 1, :] == lane, u, latest)
            lastc[0:1, :] = latest
            lastc_copy.start()
            for n in range(3):
                two = jnp.broadcast_to(tab[ROW_TWO + n: ROW_TWO + n + 1, :], (vecs, 128)) > 0
                sums = [
                    jnp.dot(
                        yt[tab_s[ROW_AT + 2 * n + t, 0]], blk[tab_s[ROW_PICK + 2 * n + t, 0]],
                        preferred_element_type=F32,
                    )
                    for t in range(2)
                ]
                t_out[n, 0] = sums[0].astype(BF16)
                t_out[n, 1] = jnp.where(two, sums[1], 0.0).astype(BF16)
            ask_copy.wait()
            for n in range(3):
                for t in range(2):
                    x_out[n, t] = xt[ask_s[n, t, 0]]
                x_backs[n].start()
            for n in range(3):
                t_sends[n].start()
            pl.semaphore_wait(all_x, 3)
            for to in lines[1]:
                pl.semaphore_signal(all_z, inc=1, device_id=(to, core), device_id_type=MESH)

        def both(i, _):
            r = c * per_pass + i
            use = [blk[r * SLOTS + s] for s in range(SLOTS)]
            prod = jnp.dot(yt[r], jnp.concatenate(use, axis=1), preferred_element_type=F32)
            lhs = [xt[tab_s[ROW_EXT + s, r]] for s in range(SLOTS)]
            kept[r] = jnp.dot(
                jnp.concatenate(lhs, axis=1),
                jnp.concatenate([block.T for block in use], axis=0),
                preferred_element_type=F32,
            )
            for s in range(SLOTS):
                summed[r * SLOTS + s] = (
                    prod[:, s * 128:(s + 1) * 128] + summed[tab_s[ROW_PREV + s, r]]
                )
            return 0

        lax.fori_loop(0, per_pass, both, 0, unroll=True)
        return 0

    lax.fori_loop(0, PASSES, one_pass, 0)

    x_send.wait()
    y_send.wait()

    def shifts(r, _):
        kept[r] += jnp.dot(
            shift_r[...], jnp.concatenate([xt[r], xo[r]], axis=0), preferred_element_type=F32
        )
        kept_l[r] = summed[tab_s[ROW_LAST, r]] + jnp.dot(
            shift_l[...], jnp.concatenate([yt[r], yo[r]], axis=0), preferred_element_type=F32
        )
        return 0

    lax.fori_loop(0, rows, shifts, 0, unroll=8)

    for n in range(3):
        x_backs[n].wait()
    fixes[6] = jnp.zeros((vecs, 128), F32)
    for u in range(6):
        fixes[u] = lax.dot_general(
            x_in[u // 2, u % 2], blk[tab_s[ROW_PICK + u, 0]], (((1,), (1,)), ((), ())),
            preferred_element_type=F32,
        ) + fixes[tab_s[ROW_SAME + u, 0]]
    def right_res(r, total):
        res = kept[r] + fixes[tab_s[ROW_FIX, r]]
        kept[r] = res
        return total + res * res

    acc[0:vecs] = lax.fori_loop(0, rows, right_res, jnp.zeros((vecs, 128), F32), unroll=8)
    right_out = pltpu.make_async_copy(kept, right_hbm, out_sem.at[0])
    right_out.start()

    lastc_copy.wait()
    back[6] = jnp.zeros((vecs, 128), F32)
    for n in range(3):
        t_sends[n].wait()
    for u in range(6):
        prev = jnp.int32(6)
        for v in range(u):
            prev = jnp.where(
                ask_s[v // 2, v % 2, 0] == ask_s[u // 2, u % 2, 0], jnp.int32(v), prev
            )
        back[u] = t_in[u // 2, u % 2].astype(F32) + back[prev]

    def left_res(c, total):
        res = kept_l[c] + back[lastc_s[0, c]]
        kept_l[c] = res
        return total + res * res

    acc[vecs: 2 * vecs] = lax.fori_loop(0, rows, left_res, jnp.zeros((vecs, 128), F32), unroll=8)
    left_out = pltpu.make_async_copy(kept_l, left_hbm, out_sem.at[1])
    left_out.start()

    mine = jnp.sum(jnp.transpose(acc[...]), axis=0, keepdims=True)
    mine = jnp.concatenate([mine, jnp.zeros((1, 128 - 2 * vecs), F32)], axis=1)
    parts[me] = mine

    def share(to):
        return pltpu.make_async_remote_copy(
            src_ref=parts.at[me], dst_ref=parts.at[me], send_sem=n_ss.at[0], recv_sem=n_rs.at[0],
            device_id=(to, core), device_id_type=MESH,
        )

    pl.semaphore_wait(all_z, 3)
    for offset in OFFSETS:
        share(peer(offset)).start()
    every = pltpu.make_async_remote_copy(
        src_ref=parts.at[pl.ds(0, peers - 1)], dst_ref=parts.at[pl.ds(0, peers - 1)],
        send_sem=n_ss.at[0], recv_sem=n_rs.at[0],
        device_id=(near[0], core), device_id_type=MESH,
    )
    every.wait_recv()
    every.wait_send()
    norm_ref[...] = jnp.sqrt(jnp.sum(parts[...], axis=0))
    right_out.wait()
    left_out.wait()


def shards(blocks, col_index, right_vecs, left_vecs, ritz):
    peers = lax.axis_size("rows")
    rows, slots = col_index.shape
    vecs, _, width = right_vecs.shape
    entries = rows * slots
    any_spec = pl.BlockSpec(memory_space=pl.ANY)
    dma = pltpu.SemaphoreType.DMA
    right, left, norms = pl.pallas_call(
        functools.partial(kernel, peers, rows, vecs),
        out_shape=(
            jax.ShapeDtypeStruct((rows, vecs, width), F32),
            jax.ShapeDtypeStruct((rows, vecs, width), F32),
            jax.ShapeDtypeStruct((1, 128), F32),
        ),
        in_specs=[any_spec] * 5,
        out_specs=(any_spec, any_spec, pl.BlockSpec(memory_space=pltpu.VMEM)),
        scratch_shapes=[
            pltpu.VMEM((slots, rows), I32),
            pltpu.VMEM((entries, width, width), BF16),
            pltpu.VMEM((2, vecs, rows, width), BF16),
            pltpu.VMEM((vecs * rows, width), F32),
            pltpu.VMEM((rows + 1, vecs, width), BF16),
            pltpu.VMEM((rows, vecs, width), BF16),
            pltpu.VMEM((rows, vecs, width), BF16),
            pltpu.VMEM((rows, vecs, width), BF16),
            pltpu.VMEM((entries + 1, vecs, width), F32),
            pltpu.VMEM((2 * vecs, 2 * vecs), BF16),
            pltpu.VMEM((vecs, 2 * vecs), BF16),
            pltpu.VMEM((vecs, 2 * vecs), BF16),
            pltpu.VMEM((48, 128), I32),
            pltpu.SMEM((48, 128), I32),
            pltpu.VMEM((3, 8, 128), I32),
            pltpu.VMEM((3, 8, 128), I32),
            pltpu.SMEM((3, 8, 128), I32),
            pltpu.VMEM((3, 2, vecs, width), BF16),
            pltpu.VMEM((3, 2, vecs, width), BF16),
            pltpu.VMEM((3, 2, vecs, width), BF16),
            pltpu.VMEM((3, 2, vecs, width), BF16),
            pltpu.VMEM((7, vecs, width), F32),
            pltpu.VMEM((7, vecs, width), F32),
            pltpu.VMEM((8, 128), I32),
            pltpu.SMEM((8, 128), I32),
            pltpu.VMEM((rows, vecs, width), F32),
            pltpu.VMEM((rows, vecs, width), F32),
            pltpu.VMEM((2 * vecs, width), F32),
            pltpu.VMEM((peers, 1, 128), F32),
            dma((4,)),
            dma((CHUNKS,)),
            dma((3,)),
            dma((2,)),
            dma((3,)), dma((3,)),
            dma((3,)), dma((3,)),
            dma((3,)), dma((3,)),
            dma((2,)), dma((2,)),
            dma((1,)), dma((1,)),
            pltpu.SemaphoreType.REGULAR, pltpu.SemaphoreType.REGULAR,
        ],
        compiler_params=pltpu.CompilerParams(
            collective_id=0, has_side_effects=True, vmem_limit_bytes=44 << 20
        ),
    )(
        *(
            pltpu.with_memory_space_constraint(arg, pltpu.HBM)
            for arg in (
                col_index.T,
                blocks.reshape(entries, width, width),
                right_vecs,
                left_vecs,
                ritz,
            )
        )
    )
    norms = norms[0, : 2 * vecs]
    return (
        jnp.swapaxes(right, 0, 1),
        jnp.swapaxes(left, 0, 1),
        norms[:vecs],
        norms[vecs:],
    )


def solution(mesh):
    placed = (
        P("rows", None, None, None),
        P("rows", None),
        P("cols", "rows", None),
        P("cols", "rows", None),
        P(),
    )
    return jax.shard_map(
        shards,
        mesh=mesh,
        in_specs=placed,
        out_specs=(P("cols", "rows", None), P("cols", "rows", None), P("cols"), P("cols")),
        check_vma=False,
    )
```

```python
import functools

import jax
import jax.numpy as jnp
from jax import lax
from jax.experimental import pallas as pl
from jax.experimental.pallas import tpu as pltpu
from jax.sharding import PartitionSpec as P

MESH = pl.DeviceIdType.MESH
F32 = jnp.float32
BF16 = jnp.bfloat16
I32 = jnp.int32
SLOTS = 7
CHUNKS = 8
PASSES = 4
OFFSETS = sorted(
    ((a, b, c) for a in range(4) for b in range(4) for c in range(4) if a + b + c),
    key=lambda d: -sum(min(v, 4 - v) for v in d),
)
ROW_EXT, ROW_PREV, ROW_LAST, ROW_PICK, ROW_TWO, ROW_SAME, ROW_FIX, ROW_AT = 0, 8, 16, 17, 24, 32, 38, 40
BACK = (1, 0, 2)


def kernel(
    peers, rows, vecs,
    cols_hbm, blocks_hbm, x_hbm, y_hbm, ritz_hbm,
    right_hbm, left_hbm, norm_ref,
    cols, blk, raw, wide, xt, yt, xo, yo, summed, ritz, shift_r, shift_l,
    tab, tab_s, ask_out, ask_in, ask_s, x_out, x_in, t_out, t_in, back, fixes, lastc, lastc_s,
    kept, kept_l, acc, parts,
    in_sem, blk_sem, loc_sem, out_sem,
    ask_ss, ask_rs, x_ss, x_rs, t_ss, t_rs, o_ss, o_rs, n_ss, n_rs, all_x, all_z,
):
    me = lax.axis_index("rows")
    core = lax.axis_index("cols")
    half = peers // 2
    entries = rows * SLOTS
    layer, place = me // half, me % half
    near = (
        layer * half + (place + 1) % half,
        layer * half + (place + half - 1) % half,
        (me + half) % peers,
    )
    other = 1 - core
    side = (me // 16, (me // 4) % 4, me % 4)

    def peer(offset):
        at = [lax.rem(a + d, 4) for a, d in zip(side, offset)]
        return at[0] * 16 + at[1] * 4 + at[2]

    barrier = pltpu.get_barrier_semaphore()
    lines = [
        [peer(tuple(d if a == axis else 0 for a in range(3))) for d in range(1, 4)]
        for axis in range(3)
    ]
    met = list(near) + lines[0] + lines[1] + lines[2]
    pl.semaphore_signal(barrier, inc=1, device_id=(me, other), device_id_type=MESH)
    for to in met:
        pl.semaphore_signal(barrier, inc=1, device_id=(to, core), device_id_type=MESH)

    ins = [
        pltpu.make_async_copy(cols_hbm, cols, in_sem.at[0]),
        pltpu.make_async_copy(y_hbm, raw.at[0], in_sem.at[1]),
        pltpu.make_async_copy(x_hbm, raw.at[1], in_sem.at[2]),
        pltpu.make_async_copy(ritz_hbm, ritz, in_sem.at[3]),
    ]
    for copy in ins:
        copy.start()
    per_chunk = entries // CHUNKS

    def chunk_copy(c):
        span = pl.ds(c * per_chunk, per_chunk)
        return pltpu.make_async_copy(blocks_hbm.at[span], blk.at[span], blk_sem.at[c])

    def start_chunk(c, _):
        chunk_copy(c).start()
        return 0

    lax.fori_loop(0, CHUNKS, start_chunk, 0)

    ins[0].wait()
    col = cols[...]
    owner = col >> 6
    local = col & 63
    row_id = lax.broadcasted_iota(I32, (SLOTS, rows), 1)
    slot_id = lax.broadcasted_iota(I32, (SLOTS, rows), 0)
    order = row_id * SLOTS + slot_id

    def all_min(v):
        return jnp.min(jnp.min(v, axis=1, keepdims=True), axis=0, keepdims=True)

    def all_max(v):
        return jnp.max(jnp.max(v, axis=1, keepdims=True), axis=0, keepdims=True)

    def put(row, value):
        tab[row: row + 1, :] = jnp.broadcast_to(value, (1, 128))

    lane = lax.broadcasted_iota(I32, (1, 128), 1)
    tab[ROW_EXT: ROW_EXT + SLOTS, :rows] = jnp.where(owner == me, local, rows)
    fix = jnp.full((1, 128), 6, I32)
    pick_rows = []
    for n in range(3):
        here = owner == near[n]
        first = all_min(jnp.where(here, order, entries))
        final = all_max(jnp.where(here, order, 0))
        picks = (first, final)
        for t in range(2):
            hit = order == picks[t]
            ask_out[n, t: t + 1, :] = jnp.broadcast_to(
                all_max(jnp.where(hit, local, 0)), (1, 128)
            )
            put(ROW_PICK + 2 * n + t, jnp.minimum(picks[t], entries - 1))
            at = all_max(jnp.where(hit, row_id, 0))
            put(ROW_AT + 2 * n + t, at)
            if t == 1:
                at = jnp.where(first == final, -1, at)
            same = jnp.full((1, 1), 6, I32)
            for v, earlier in enumerate(pick_rows):
                same = jnp.where(earlier == at, v, same)
            put(ROW_SAME + 2 * n + t, same)
            fix = jnp.where(lane == at, 2 * n + t, fix)
            pick_rows.append(at)
        ask_out[n, 2:8, :] = jnp.zeros((6, 128), I32)
        put(ROW_TWO + n, (first != final).astype(I32))
    put(ROW_FIX, fix)

    asks = [
        pltpu.make_async_remote_copy(
            src_ref=ask_out.at[n], dst_ref=ask_in.at[BACK[n]],
            send_sem=ask_ss.at[n], recv_sem=ask_rs.at[BACK[n]],
            device_id=(near[n], core), device_id_type=MESH,
        )
        for n in range(3)
    ]

    col_t = jnp.transpose(
        jnp.concatenate([col.astype(F32), jnp.full((1, rows), -1.0, F32)], axis=0)
    ).astype(I32)
    src_row = lax.broadcasted_iota(I32, (rows, rows), 0)
    dst_row = lax.broadcasted_iota(I32, (rows, rows), 1)
    before, upto = src_row < dst_row, src_row <= dst_row
    src_order = src_row * SLOTS
    src_col = [jnp.broadcast_to(col_t[:, s:s + 1], (rows, rows)) for s in range(SLOTS)]
    for s in range(SLOTS):
        mine = jnp.broadcast_to(col[s:s + 1, :], (rows, rows))
        best = jnp.full((rows, rows), -1, I32)
        for t in range(SLOTS):
            best = jnp.where(
                (src_col[t] == mine) & (upto if t < s else before), src_order + t, best
            )
        found = jnp.max(best, axis=0, keepdims=True)
        found = jnp.where((found < 0) | (owner[s:s + 1, :] != me), entries, found)
        tab[ROW_PREV + s: ROW_PREV + s + 1, :rows] = found
    best = jnp.full((rows, rows), 0, I32)
    for t in range(SLOTS):
        best = jnp.where(src_col[t] == dst_row + me * rows, src_order + t, best)
    tab[ROW_LAST: ROW_LAST + 1, :rows] = jnp.max(best, axis=0, keepdims=True)
    tab_copy = pltpu.make_async_copy(tab, tab_s, loc_sem.at[0])
    tab_copy.start()

    def by_rows(index, dst):
        def widen(k, _):
            wide[pl.ds(k * rows, rows), :] = raw[index, k].astype(F32)
            return 0

        lax.fori_loop(0, vecs, widen, 0, unroll=4)

        def turn(r, _):
            dst[r] = wide[pl.ds(r, vecs, stride=rows), :].astype(BF16)
            return 0

        lax.fori_loop(0, rows, turn, 0, unroll=8)

    def across(src, dst, slot):
        return pltpu.make_async_remote_copy(
            src_ref=src, dst_ref=dst, send_sem=o_ss.at[slot], recv_sem=o_rs.at[slot],
            device_id=(me, other), device_id_type=MESH,
        )

    ins[1].wait()
    by_rows(0, yt)
    y_send = across(yt, yo, 0)
    pl.semaphore_wait(barrier, len(met) + 1)
    for copy in asks:
        copy.start()
    for to in lines[0]:
        pl.semaphore_signal(all_x, inc=1, device_id=(to, core), device_id_type=MESH)
    y_send.start()
    ins[2].wait()
    by_rows(1, xt)
    x_send = across(xt.at[pl.ds(0, rows)], xo, 1)
    x_send.start()

    ins[3].wait()
    table = ritz[...].astype(F32)
    low = core == 0
    picked = jnp.where(low, table[:, :vecs], table[:, vecs:])
    picked = jnp.concatenate(
        [jnp.where(low, picked[:vecs], picked[vecs:]), jnp.where(low, picked[vecs:], picked[:vecs])],
        axis=0,
    )
    shift_r[...] = (-jnp.transpose(picked)).astype(BF16)
    picked = jnp.where(low, table[:vecs], table[vecs:])
    picked = jnp.concatenate(
        [
            jnp.where(low, picked[:, :vecs], picked[:, vecs:]),
            jnp.where(low, picked[:, vecs:], picked[:, :vecs]),
        ],
        axis=1,
    )
    shift_l[...] = (-picked).astype(BF16)
    summed[entries] = jnp.zeros((vecs, 128), F32)

    x_backs = [
        pltpu.make_async_remote_copy(
            src_ref=x_out.at[n], dst_ref=x_in.at[BACK[n]],
            send_sem=x_ss.at[n], recv_sem=x_rs.at[BACK[n]],
            device_id=(near[n], core), device_id_type=MESH,
        )
        for n in range(3)
    ]

    xt[rows] = jnp.zeros((vecs, 128), BF16)
    tab_copy.wait()

    per_pass = rows // PASSES

    ask_copy = pltpu.make_async_copy(ask_in, ask_s, loc_sem.at[1])
    lastc_copy = pltpu.make_async_copy(lastc, lastc_s, loc_sem.at[2])
    t_sends = [
        pltpu.make_async_remote_copy(
            src_ref=t_out.at[n], dst_ref=t_in.at[BACK[n]],
            send_sem=t_ss.at[n], recv_sem=t_rs.at[BACK[n]],
            device_id=(near[n], core), device_id_type=MESH,
        )
        for n in range(3)
    ]

    def one_pass(c, _):
        for half_pass in range(CHUNKS // PASSES):
            chunk_copy(c * (CHUNKS // PASSES) + half_pass).wait()

        @pl.when(c == PASSES - 1)
        def _():
            for n in range(3):
                two = jnp.broadcast_to(tab[ROW_TWO + n: ROW_TWO + n + 1, :], (vecs, 128)) > 0
                sums = [
                    jnp.dot(
                        yt[tab_s[ROW_AT + 2 * n + t, 0]], blk[tab_s[ROW_PICK + 2 * n + t, 0]],
                        preferred_element_type=F32,
                    )
                    for t in range(2)
                ]
                t_out[n, 0] = sums[0].astype(BF16)
                t_out[n, 1] = jnp.where(two, sums[1], 0.0).astype(BF16)
            for n in range(3):
                t_sends[n].start()
            for n in range(3):
                asks[n].wait()
            for n in range(3):
                for t in range(2):
                    x_out[n, t] = xt[ask_in[n, t, 0]]
                x_backs[n].start()
            ask_copy.start()
            latest = jnp.full((1, 128), 6, I32)
            for u in range(6):
                latest = jnp.where(ask_in[u // 2, u % 2: u % 2 + 1, :] == lane, u, latest)
            lastc[0:1, :] = latest
            lastc_copy.start()
            pl.semaphore_wait(all_x, 3)
            for to in lines[1]:
                pl.semaphore_signal(all_z, inc=1, device_id=(to, core), device_id_type=MESH)

        def both(i, _):
            r = c * per_pass + i
            use = [blk[r * SLOTS + s] for s in range(SLOTS)]
            prod = jnp.dot(yt[r], jnp.concatenate(use, axis=1), preferred_element_type=F32)
            lhs = [xt[tab_s[ROW_EXT + s, r]] for s in range(SLOTS)]
            kept[r] = jnp.dot(
                jnp.concatenate(lhs, axis=1),
                jnp.concatenate([block.T for block in use], axis=0),
                preferred_element_type=F32,
            )
            for s in range(SLOTS):
                summed[r * SLOTS + s] = (
                    prod[:, s * 128:(s + 1) * 128] + summed[tab_s[ROW_PREV + s, r]]
                )
            return 0

        lax.fori_loop(0, per_pass, both, 0, unroll=True)
        return 0

    lax.fori_loop(0, PASSES, one_pass, 0)

    x_send.wait()
    y_send.wait()

    def shifts(r, _):
        kept[r] += jnp.dot(
            shift_r[...], jnp.concatenate([xt[r], xo[r]], axis=0), preferred_element_type=F32
        )
        kept_l[r] = summed[tab_s[ROW_LAST, r]] + jnp.dot(
            shift_l[...], jnp.concatenate([yt[r], yo[r]], axis=0), preferred_element_type=F32
        )
        return 0

    lax.fori_loop(0, rows, shifts, 0, unroll=8)

    for n in range(3):
        x_backs[n].wait()
    fixes[6] = jnp.zeros((vecs, 128), F32)
    for u in range(6):
        fixes[u] = lax.dot_general(
            x_in[u // 2, u % 2], blk[tab_s[ROW_PICK + u, 0]], (((1,), (1,)), ((), ())),
            preferred_element_type=F32,
        ) + fixes[tab_s[ROW_SAME + u, 0]]
    def right_res(r, total):
        res = kept[r] + fixes[tab_s[ROW_FIX, r]]
        kept[r] = res
        return total + res * res

    acc[0:vecs] = lax.fori_loop(0, rows, right_res, jnp.zeros((vecs, 128), F32), unroll=8)

    lastc_copy.wait()
    ask_copy.wait()
    back[6] = jnp.zeros((vecs, 128), F32)
    for n in range(3):
        t_sends[n].wait()
    for u in range(6):
        prev = jnp.int32(6)
        for v in range(u):
            prev = jnp.where(
                ask_s[v // 2, v % 2, 0] == ask_s[u // 2, u % 2, 0], jnp.int32(v), prev
            )
        back[u] = t_in[u // 2, u % 2].astype(F32) + back[prev]

    def left_res(c, total):
        res = kept_l[c] + back[lastc_s[0, c]]
        kept_l[c] = res
        return total + res * res

    acc[vecs: 2 * vecs] = lax.fori_loop(0, rows, left_res, jnp.zeros((vecs, 128), F32), unroll=8)

    mine = jnp.sum(jnp.transpose(acc[...]), axis=0, keepdims=True)
    mine = jnp.concatenate([mine, jnp.zeros((1, 128 - 2 * vecs), F32)], axis=1)
    parts[me] = mine

    def share(to):
        return pltpu.make_async_remote_copy(
            src_ref=parts.at[me], dst_ref=parts.at[me], send_sem=n_ss.at[0], recv_sem=n_rs.at[0],
            device_id=(to, core), device_id_type=MESH,
        )

    pl.semaphore_wait(all_z, 3)
    for offset in OFFSETS:
        share(peer(offset)).start()
    every = pltpu.make_async_remote_copy(
        src_ref=parts.at[pl.ds(0, peers - 1)], dst_ref=parts.at[pl.ds(0, peers - 1)],
        send_sem=n_ss.at[0], recv_sem=n_rs.at[0],
        device_id=(near[0], core), device_id_type=MESH,
    )

    def store(r, _):
        pltpu.make_async_copy(kept.at[r], right_hbm.at[:, r, 0], out_sem.at[0]).start()
        pltpu.make_async_copy(kept_l.at[r], left_hbm.at[:, r, 0], out_sem.at[1]).start()
        return 0

    lax.fori_loop(0, rows, store, 0, unroll=4)
    every.wait_recv()
    every.wait_send()
    norm_ref[...] = jnp.sqrt(jnp.sum(parts[...], axis=0))
    pltpu.make_async_copy(kept, kept, out_sem.at[0]).wait()
    pltpu.make_async_copy(kept_l, kept_l, out_sem.at[1]).wait()


def finish(right, left, norms, right_out, left_out, right_norms, left_norms, sem):
    copies = [
        pltpu.make_async_copy(right, right_out, sem.at[0]),
        pltpu.make_async_copy(left, left_out, sem.at[1]),
    ]
    for copy in copies:
        copy.start()
    half = right_norms.shape[0]
    right_norms[...] = norms[0, :half]
    left_norms[...] = norms[0, half: 2 * half]
    for copy in copies:
        copy.wait()


def shards(blocks, col_index, right_vecs, left_vecs, ritz):
    peers = lax.axis_size("rows")
    rows, slots = col_index.shape
    vecs, _, width = right_vecs.shape
    entries = rows * slots
    any_spec = pl.BlockSpec(memory_space=pl.ANY)
    dma = pltpu.SemaphoreType.DMA
    right, left, norms = pl.pallas_call(
        functools.partial(kernel, peers, rows, vecs),
        out_shape=(
            jax.ShapeDtypeStruct((vecs, rows, 1, width), F32),
            jax.ShapeDtypeStruct((vecs, rows, 1, width), F32),
            jax.ShapeDtypeStruct((1, 128), F32),
        ),
        in_specs=[any_spec] * 5,
        out_specs=(any_spec, any_spec, pl.BlockSpec(memory_space=pltpu.VMEM)),
        scratch_shapes=[
            pltpu.VMEM((slots, rows), I32),
            pltpu.VMEM((entries, width, width), BF16),
            pltpu.VMEM((2, vecs, rows, width), BF16),
            pltpu.VMEM((vecs * rows, width), F32),
            pltpu.VMEM((rows + 1, vecs, width), BF16),
            pltpu.VMEM((rows, vecs, width), BF16),
            pltpu.VMEM((rows, vecs, width), BF16),
            pltpu.VMEM((rows, vecs, width), BF16),
            pltpu.VMEM((entries + 1, vecs, width), F32),
            pltpu.VMEM((2 * vecs, 2 * vecs), BF16),
            pltpu.VMEM((vecs, 2 * vecs), BF16),
            pltpu.VMEM((vecs, 2 * vecs), BF16),
            pltpu.VMEM((48, 128), I32),
            pltpu.SMEM((48, 128), I32),
            pltpu.VMEM((3, 8, 128), I32),
            pltpu.VMEM((3, 8, 128), I32),
            pltpu.SMEM((3, 8, 128), I32),
            pltpu.VMEM((3, 2, vecs, width), BF16),
            pltpu.VMEM((3, 2, vecs, width), BF16),
            pltpu.VMEM((3, 2, vecs, width), BF16),
            pltpu.VMEM((3, 2, vecs, width), BF16),
            pltpu.VMEM((7, vecs, width), F32),
            pltpu.VMEM((7, vecs, width), F32),
            pltpu.VMEM((8, 128), I32),
            pltpu.SMEM((8, 128), I32),
            pltpu.VMEM((rows, vecs, width), F32),
            pltpu.VMEM((rows, vecs, width), F32),
            pltpu.VMEM((2 * vecs, width), F32),
            pltpu.VMEM((peers, 1, 128), F32),
            dma((4,)),
            dma((CHUNKS,)),
            dma((3,)),
            dma((2,)),
            dma((3,)), dma((3,)),
            dma((3,)), dma((3,)),
            dma((3,)), dma((3,)),
            dma((2,)), dma((2,)),
            dma((1,)), dma((1,)),
            pltpu.SemaphoreType.REGULAR, pltpu.SemaphoreType.REGULAR,
        ],
        compiler_params=pltpu.CompilerParams(
            collective_id=0, has_side_effects=True, vmem_limit_bytes=44 << 20
        ),
    )(
        *(
            pltpu.with_memory_space_constraint(arg, pltpu.HBM)
            for arg in (
                col_index.T,
                blocks.reshape(entries, width, width),
                right_vecs,
                left_vecs,
                ritz,
            )
        )
    )
    vmem = pl.BlockSpec(memory_space=pltpu.VMEM)
    return pl.pallas_call(
        finish,
        out_shape=(
            jax.ShapeDtypeStruct((vecs, rows, width), F32),
            jax.ShapeDtypeStruct((vecs, rows, width), F32),
            jax.ShapeDtypeStruct((vecs,), F32),
            jax.ShapeDtypeStruct((vecs,), F32),
        ),
        in_specs=[vmem] * 3,
        out_specs=(any_spec, any_spec, vmem, vmem),
        scratch_shapes=[dma((2,))],
        compiler_params=pltpu.CompilerParams(vmem_limit_bytes=8 << 20),
    )(right.reshape(vecs, rows, width), left.reshape(vecs, rows, width), norms)


def solution(mesh):
    placed = (
        P("rows", None, None, None),
        P("rows", None),
        P("cols", "rows", None),
        P("cols", "rows", None),
        P(),
    )
    return jax.shard_map(
        shards,
        mesh=mesh,
        in_specs=placed,
        out_specs=(P("cols", "rows", None), P("cols", "rows", None), P("cols"), P("cols")),
        check_vma=False,
    )
```

```python
import functools

import jax
import jax.numpy as jnp
from jax import lax
from jax.experimental import pallas as pl
from jax.experimental.pallas import tpu as pltpu
from jax.sharding import PartitionSpec as P

MESH = pl.DeviceIdType.MESH
F32 = jnp.float32
BF16 = jnp.bfloat16
I32 = jnp.int32
SLOTS = 7
CHUNKS = 8
SERVE = 5
OFFSETS = sorted(
    ((a, b, c) for a in range(4) for b in range(4) for c in range(4) if a + b + c),
    key=lambda d: -sum(min(v, 4 - v) for v in d),
)
ROW_EXT, ROW_PREV, ROW_LAST, ROW_PICK, ROW_TWO, ROW_SAME, ROW_FIX, ROW_AT = 0, 8, 16, 17, 24, 32, 38, 40
BACK = (1, 0, 2)


def kernel(
    peers, rows, vecs,
    cols_hbm, blocks_hbm, x_hbm, y_hbm, ritz_hbm,
    right, left, norm_ref,
    cols, blk, raw, wide, xt, yt, xo, yo, summed, ritz, shift_r, shift_l,
    tab, tab_s, ask_out, ask_in, ask_s, x_out, x_in, t_out, t_in, back, fixes, lastc, lastc_s,
    kept, kept_l, turned, parts,
    in_sem, blk_sem, loc_sem,
    ask_ss, ask_rs, x_ss, x_rs, t_ss, t_rs, o_ss, o_rs, n_ss, n_rs, all_x, all_z,
):
    me = lax.axis_index("rows")
    core = lax.axis_index("cols")
    half = peers // 2
    entries = rows * SLOTS
    layer, place = me // half, me % half
    near = (
        layer * half + (place + 1) % half,
        layer * half + (place + half - 1) % half,
        (me + half) % peers,
    )
    other = 1 - core
    side = (me // 16, (me // 4) % 4, me % 4)

    def peer(offset):
        at = [lax.rem(a + d, 4) for a, d in zip(side, offset)]
        return at[0] * 16 + at[1] * 4 + at[2]

    barrier = pltpu.get_barrier_semaphore()
    lines = [
        [peer(tuple(d if a == axis else 0 for a in range(3))) for d in range(1, 4)]
        for axis in range(3)
    ]
    met = list(near) + lines[0] + lines[1] + lines[2]
    pl.semaphore_signal(barrier, inc=1, device_id=(me, other), device_id_type=MESH)
    for to in met:
        pl.semaphore_signal(barrier, inc=1, device_id=(to, core), device_id_type=MESH)

    ins = [
        pltpu.make_async_copy(cols_hbm, cols, in_sem.at[0]),
        pltpu.make_async_copy(y_hbm, raw.at[0], in_sem.at[1]),
        pltpu.make_async_copy(x_hbm, raw.at[1], in_sem.at[2]),
        pltpu.make_async_copy(ritz_hbm, ritz, in_sem.at[3]),
    ]
    for copy in ins:
        copy.start()
    per_chunk = entries // CHUNKS

    def chunk_copy(c):
        span = pl.ds(c * per_chunk, per_chunk)
        return pltpu.make_async_copy(blocks_hbm.at[span], blk.at[span], blk_sem.at[c])

    def start_chunk(c, _):
        chunk_copy(c).start()
        return 0

    lax.fori_loop(0, CHUNKS, start_chunk, 0)

    ins[0].wait()
    col = cols[...]
    owner = col >> 6
    local = col & 63
    row_id = lax.broadcasted_iota(I32, (SLOTS, rows), 1)
    slot_id = lax.broadcasted_iota(I32, (SLOTS, rows), 0)
    order = row_id * SLOTS + slot_id

    def all_min(v):
        return jnp.min(jnp.min(v, axis=1, keepdims=True), axis=0, keepdims=True)

    def all_max(v):
        return jnp.max(jnp.max(v, axis=1, keepdims=True), axis=0, keepdims=True)

    def put(row, value):
        tab[row: row + 1, :] = jnp.broadcast_to(value, (1, 128))

    lane = lax.broadcasted_iota(I32, (1, 128), 1)
    tab[ROW_EXT: ROW_EXT + SLOTS, :rows] = jnp.where(owner == me, local, rows)
    fix = jnp.full((1, 128), 6, I32)
    pick_rows = []
    for n in range(3):
        here = owner == near[n]
        first = all_min(jnp.where(here, order, entries))
        final = all_max(jnp.where(here, order, 0))
        picks = (first, final)
        for t in range(2):
            hit = order == picks[t]
            ask_out[n, t: t + 1, :] = jnp.broadcast_to(
                all_max(jnp.where(hit, local, 0)), (1, 128)
            )
            put(ROW_PICK + 2 * n + t, jnp.minimum(picks[t], entries - 1))
            at = all_max(jnp.where(hit, row_id, 0))
            put(ROW_AT + 2 * n + t, at)
            if t == 1:
                at = jnp.where(first == final, -1, at)
            same = jnp.full((1, 1), 6, I32)
            for v, earlier in enumerate(pick_rows):
                same = jnp.where(earlier == at, v, same)
            put(ROW_SAME + 2 * n + t, same)
            fix = jnp.where(lane == at, 2 * n + t, fix)
            pick_rows.append(at)
        ask_out[n, 2:8, :] = jnp.zeros((6, 128), I32)
        put(ROW_TWO + n, (first != final).astype(I32))
    put(ROW_FIX, fix)

    asks = [
        pltpu.make_async_remote_copy(
            src_ref=ask_out.at[n], dst_ref=ask_in.at[BACK[n]],
            send_sem=ask_ss.at[n], recv_sem=ask_rs.at[BACK[n]],
            device_id=(near[n], core), device_id_type=MESH,
        )
        for n in range(3)
    ]

    col_t = jnp.transpose(
        jnp.concatenate([col.astype(F32), jnp.full((1, rows), -1.0, F32)], axis=0)
    ).astype(I32)
    src_row = lax.broadcasted_iota(I32, (rows, rows), 0)
    dst_row = lax.broadcasted_iota(I32, (rows, rows), 1)
    before, upto = src_row < dst_row, src_row <= dst_row
    src_order = src_row * SLOTS
    src_col = [jnp.broadcast_to(col_t[:, s:s + 1], (rows, rows)) for s in range(SLOTS)]
    for s in range(SLOTS):
        mine = jnp.broadcast_to(col[s:s + 1, :], (rows, rows))
        best = jnp.full((rows, rows), -1, I32)
        for t in range(SLOTS):
            best = jnp.where(
                (src_col[t] == mine) & (upto if t < s else before), src_order + t, best
            )
        found = jnp.max(best, axis=0, keepdims=True)
        found = jnp.where((found < 0) | (owner[s:s + 1, :] != me), entries, found)
        tab[ROW_PREV + s: ROW_PREV + s + 1, :rows] = found
    best = jnp.full((rows, rows), 0, I32)
    for t in range(SLOTS):
        best = jnp.where(src_col[t] == dst_row + me * rows, src_order + t, best)
    tab[ROW_LAST: ROW_LAST + 1, :rows] = jnp.max(best, axis=0, keepdims=True)
    tab_copy = pltpu.make_async_copy(tab, tab_s, loc_sem.at[0])
    tab_copy.start()

    def by_rows(index, dst):
        def widen(k, _):
            wide[pl.ds(k * rows, rows), :] = raw[index, k].astype(F32)
            return 0

        lax.fori_loop(0, vecs, widen, 0, unroll=4)

        def turn(r, _):
            dst[r] = wide[pl.ds(r, vecs, stride=rows), :].astype(BF16)
            return 0

        lax.fori_loop(0, rows, turn, 0, unroll=8)

    def across(src, dst, slot):
        return pltpu.make_async_remote_copy(
            src_ref=src, dst_ref=dst, send_sem=o_ss.at[slot], recv_sem=o_rs.at[slot],
            device_id=(me, other), device_id_type=MESH,
        )

    ins[1].wait()
    by_rows(0, yt)
    y_send = across(yt, yo, 0)
    ins[2].wait()
    by_rows(1, xt)
    x_send = across(xt.at[pl.ds(0, rows)], xo, 1)
    pl.semaphore_wait(barrier, len(met) + 1)
    for copy in asks:
        copy.start()
    for to in lines[0]:
        pl.semaphore_signal(all_x, inc=1, device_id=(to, core), device_id_type=MESH)
    y_send.start()
    x_send.start()

    ins[3].wait()
    table = ritz[...].astype(F32)
    low = core == 0
    picked = jnp.where(low, table[:, :vecs], table[:, vecs:])
    picked = jnp.concatenate(
        [jnp.where(low, picked[:vecs], picked[vecs:]), jnp.where(low, picked[vecs:], picked[:vecs])],
        axis=0,
    )
    shift_r[...] = (-jnp.transpose(picked)).astype(BF16)
    picked = jnp.where(low, table[:vecs], table[vecs:])
    picked = jnp.concatenate(
        [
            jnp.where(low, picked[:, :vecs], picked[:, vecs:]),
            jnp.where(low, picked[:, vecs:], picked[:, :vecs]),
        ],
        axis=1,
    )
    shift_l[...] = (-picked).astype(BF16)
    summed[entries] = jnp.zeros((vecs, 128), F32)

    x_backs = [
        pltpu.make_async_remote_copy(
            src_ref=x_out.at[n], dst_ref=x_in.at[BACK[n]],
            send_sem=x_ss.at[n], recv_sem=x_rs.at[BACK[n]],
            device_id=(near[n], core), device_id_type=MESH,
        )
        for n in range(3)
    ]

    xt[rows] = jnp.zeros((vecs, 128), BF16)
    tab_copy.wait()

    per_pass = rows // 4

    ask_copy = pltpu.make_async_copy(ask_in, ask_s, loc_sem.at[1])
    lastc_copy = pltpu.make_async_copy(lastc, lastc_s, loc_sem.at[2])
    t_sends = [
        pltpu.make_async_remote_copy(
            src_ref=t_out.at[n], dst_ref=t_in.at[BACK[n]],
            send_sem=t_ss.at[n], recv_sem=t_rs.at[BACK[n]],
            device_id=(near[n], core), device_id_type=MESH,
        )
        for n in range(3)
    ]

    def one_pass(c, _):
        @pl.when(c < 3)
        def _():
            chunk_copy(2 * c).wait()
            chunk_copy(2 * c + 1).wait()

        @pl.when(c == 3)
        def _():
            for last in range(6, CHUNKS):
                chunk_copy(last).wait()
            for n in range(3):
                two = jnp.broadcast_to(tab[ROW_TWO + n: ROW_TWO + n + 1, :], (vecs, 128)) > 0
                sums = [
                    jnp.dot(
                        yt[tab_s[ROW_AT + 2 * n + t, 0]], blk[tab_s[ROW_PICK + 2 * n + t, 0]],
                        preferred_element_type=F32,
                    )
                    for t in range(2)
                ]
                t_out[n, 0] = sums[0].astype(BF16)
                t_out[n, 1] = jnp.where(two, sums[1], 0.0).astype(BF16)
            for n in range(3):
                t_sends[n].start()
            for n in range(3):
                asks[n].wait()
            for n in range(3):
                for t in range(2):
                    x_out[n, t] = xt[ask_in[n, t, 0]]
                x_backs[n].start()
            ask_copy.start()
            latest = jnp.full((1, 128), 6, I32)
            for u in range(6):
                latest = jnp.where(ask_in[u // 2, u % 2: u % 2 + 1, :] == lane, u, latest)
            lastc[0:1, :] = latest
            lastc_copy.start()
            pl.semaphore_wait(all_x, 3)
            for to in lines[1]:
                pl.semaphore_signal(all_z, inc=1, device_id=(to, core), device_id_type=MESH)

        def both(i, _):
            r = c * per_pass + i
            use = [blk[r * SLOTS + s] for s in range(SLOTS)]
            prod = jnp.dot(yt[r], jnp.concatenate(use, axis=1), preferred_element_type=F32)
            lhs = [xt[tab_s[ROW_EXT + s, r]] for s in range(SLOTS)]
            kept[r] = jnp.dot(
                jnp.concatenate(lhs, axis=1),
                jnp.concatenate([block.T for block in use], axis=0),
                preferred_element_type=F32,
            )
            for s in range(SLOTS):
                summed[r * SLOTS + s] = (
                    prod[:, s * 128:(s + 1) * 128] + summed[tab_s[ROW_PREV + s, r]]
                )
            return 0

        lax.fori_loop(0, per_pass, both, 0, unroll=True)
        return 0

    lax.fori_loop(0, 4, one_pass, 0)

    x_send.wait()
    y_send.wait()

    lastc_copy.wait()
    ask_copy.wait()

    def shifts(r, totals):
        res = kept[r] + jnp.dot(
            shift_r[...], jnp.concatenate([xt[r], xo[r]], axis=0), preferred_element_type=F32
        )
        kept[r] = res
        res_l = summed[tab_s[ROW_LAST, r]] + jnp.dot(
            shift_l[...], jnp.concatenate([yt[r], yo[r]], axis=0), preferred_element_type=F32
        )
        kept_l[r] = res_l
        return (
            totals[0] + jnp.where(tab_s[ROW_FIX, r] == 6, res * res, 0.0),
            totals[1] + jnp.where(lastc_s[0, r] == 6, res_l * res_l, 0.0),
        )

    zero = jnp.zeros((vecs, 128), F32)
    right_sq, left_sq = lax.fori_loop(0, rows, shifts, (zero, zero), unroll=16)
    for u in range(6):
        turned[u] = blk[tab_s[ROW_PICK + u, 0]].T

    for n in range(3):
        x_backs[n].wait()
    fixes[6] = zero
    for u in range(6):
        fix = fixes[tab_s[ROW_SAME + u, 0]] + jnp.dot(
            x_in[u // 2, u % 2], turned[u], preferred_element_type=F32
        )
        fixes[u] = fix
        at = tab_s[ROW_AT + u, 0]
        res = kept[at] + fix
        right_sq += jnp.where(tab_s[ROW_FIX, at] == u, res * res, 0.0)

    back[6] = zero
    for n in range(3):
        t_sends[n].wait()
    for u in range(6):
        prev = jnp.int32(6)
        for v in range(u):
            prev = jnp.where(
                ask_s[v // 2, v % 2, 0] == ask_s[u // 2, u % 2, 0], jnp.int32(v), prev
            )
        back[u] = t_in[u // 2, u % 2].astype(F32) + back[prev]
        at = ask_s[u // 2, u % 2, 0]
        res = kept_l[at] + back[u]
        left_sq += jnp.where(lastc_s[0, at] == u, res * res, 0.0)

    mine = jnp.concatenate([right_sq, left_sq], axis=0)
    mine = jnp.sum(jnp.transpose(mine), axis=0, keepdims=True)
    mine = jnp.concatenate([mine, jnp.zeros((1, 128 - 2 * vecs), F32)], axis=1)
    parts[me] = mine

    def share(to):
        return pltpu.make_async_remote_copy(
            src_ref=parts.at[me], dst_ref=parts.at[me], send_sem=n_ss.at[0], recv_sem=n_rs.at[0],
            device_id=(to, core), device_id_type=MESH,
        )

    pl.semaphore_wait(all_z, 3)
    for offset in OFFSETS:
        share(peer(offset)).start()
    every = pltpu.make_async_remote_copy(
        src_ref=parts.at[pl.ds(0, peers - 1)], dst_ref=parts.at[pl.ds(0, peers - 1)],
        send_sem=n_ss.at[0], recv_sem=n_rs.at[0],
        device_id=(near[0], core), device_id_type=MESH,
    )

    def store(r, _):
        right[pl.ds(r, vecs, stride=rows), :] = kept[r] + fixes[tab_s[ROW_FIX, r]]
        left[pl.ds(r, vecs, stride=rows), :] = kept_l[r] + back[lastc_s[0, r]]
        return 0

    lax.fori_loop(0, rows, store, 0, unroll=8)
    every.wait_recv()
    every.wait_send()
    norm_ref[...] = jnp.sqrt(jnp.sum(parts[...], axis=0))


def finish(right, left, norms, right_out, left_out, right_norms, left_norms, first, second, sem):
    half = right_norms.shape[0]
    copies = [
        pltpu.make_async_copy(right, right_out, sem.at[0]),
        pltpu.make_async_copy(left, left_out, sem.at[1]),
        pltpu.make_async_copy(first, right_norms, sem.at[2]),
        pltpu.make_async_copy(second, left_norms, sem.at[3]),
    ]
    copies[0].start()
    copies[1].start()
    first[...] = norms[0, :half]
    second[...] = norms[0, half: 2 * half]
    copies[2].start()
    copies[3].start()
    for copy in copies:
        copy.wait()


def shards(blocks, col_index, right_vecs, left_vecs, ritz):
    peers = lax.axis_size("rows")
    rows, slots = col_index.shape
    vecs, _, width = right_vecs.shape
    entries = rows * slots
    any_spec = pl.BlockSpec(memory_space=pl.ANY)
    vmem = pl.BlockSpec(memory_space=pltpu.VMEM)
    dma = pltpu.SemaphoreType.DMA
    right, left, norms = pl.pallas_call(
        functools.partial(kernel, peers, rows, vecs),
        out_shape=(
            jax.ShapeDtypeStruct((vecs * rows, width), F32),
            jax.ShapeDtypeStruct((vecs * rows, width), F32),
            jax.ShapeDtypeStruct((1, 128), F32),
        ),
        in_specs=[any_spec] * 5,
        out_specs=(vmem,) * 3,
        scratch_shapes=[
            pltpu.VMEM((slots, rows), I32),
            pltpu.VMEM((entries, width, width), BF16),
            pltpu.VMEM((2, vecs, rows, width), BF16),
            pltpu.VMEM((vecs * rows, width), F32),
            pltpu.VMEM((rows + 1, vecs, width), BF16),
            pltpu.VMEM((rows, vecs, width), BF16),
            pltpu.VMEM((rows, vecs, width), BF16),
            pltpu.VMEM((rows, vecs, width), BF16),
            pltpu.VMEM((entries + 1, vecs, width), F32),
            pltpu.VMEM((2 * vecs, 2 * vecs), BF16),
            pltpu.VMEM((vecs, 2 * vecs), BF16),
            pltpu.VMEM((vecs, 2 * vecs), BF16),
            pltpu.VMEM((48, 128), I32),
            pltpu.SMEM((48, 128), I32),
            pltpu.VMEM((3, 8, 128), I32),
            pltpu.VMEM((3, 8, 128), I32),
            pltpu.SMEM((3, 8, 128), I32),
            pltpu.VMEM((3, 2, vecs, width), BF16),
            pltpu.VMEM((3, 2, vecs, width), BF16),
            pltpu.VMEM((3, 2, vecs, width), BF16),
            pltpu.VMEM((3, 2, vecs, width), BF16),
            pltpu.VMEM((7, vecs, width), F32),
            pltpu.VMEM((7, vecs, width), F32),
            pltpu.VMEM((8, 128), I32),
            pltpu.SMEM((8, 128), I32),
            pltpu.VMEM((rows, vecs, width), F32),
            pltpu.VMEM((rows, vecs, width), F32),
            pltpu.VMEM((6, width, width), BF16),
            pltpu.VMEM((peers, 1, 128), F32),
            dma((4,)),
            dma((CHUNKS,)),
            dma((3,)),
            dma((3,)), dma((3,)),
            dma((3,)), dma((3,)),
            dma((3,)), dma((3,)),
            dma((2,)), dma((2,)),
            dma((1,)), dma((1,)),
            pltpu.SemaphoreType.REGULAR, pltpu.SemaphoreType.REGULAR,
        ],
        compiler_params=pltpu.CompilerParams(
            collective_id=0, has_side_effects=True, vmem_limit_bytes=44 << 20
        ),
    )(
        *(
            pltpu.with_memory_space_constraint(arg, pltpu.HBM)
            for arg in (
                col_index.T,
                blocks.reshape(entries, width, width),
                right_vecs,
                left_vecs,
                ritz,
            )
        )
    )
    return pl.pallas_call(
        finish,
        out_shape=(
            jax.ShapeDtypeStruct((vecs, rows, width), F32),
            jax.ShapeDtypeStruct((vecs, rows, width), F32),
            jax.ShapeDtypeStruct((vecs,), F32),
            jax.ShapeDtypeStruct((vecs,), F32),
        ),
        in_specs=[vmem] * 3,
        out_specs=(any_spec,) * 4,
        scratch_shapes=[pltpu.VMEM((vecs,), F32), pltpu.VMEM((vecs,), F32), dma((4,))],
        compiler_params=pltpu.CompilerParams(vmem_limit_bytes=8 << 20),
    )(right.reshape(vecs, rows, width), left.reshape(vecs, rows, width), norms)


def solution(mesh):
    placed = (
        P("rows", None, None, None),
        P("rows", None),
        P("cols", "rows", None),
        P("cols", "rows", None),
        P(),
    )
    return jax.shard_map(
        shards,
        mesh=mesh,
        in_specs=placed,
        out_specs=(P("cols", "rows", None), P("cols", "rows", None), P("cols"), P("cols")),
        check_vma=False,
    )
```

```python
import functools

import jax
import jax.numpy as jnp
from jax import lax
from jax.experimental import pallas as pl
from jax.experimental.pallas import tpu as pltpu
from jax.sharding import PartitionSpec as P

MESH = pl.DeviceIdType.MESH
F32 = jnp.float32
BF16 = jnp.bfloat16
I32 = jnp.int32
SLOTS = 7
CHUNKS = 8
ORDER = sorted(range(64), key=lambda p: (p // 16 + p // 4 % 4 + p % 4, p))
ROW_EXT, ROW_PREV, ROW_LAST, ROW_PICK, ROW_TWO, ROW_SAME, ROW_FIX, ROW_AT = 0, 8, 16, 17, 24, 32, 38, 40
BACK = (1, 0, 2)


def kernel(
    peers, rows, vecs,
    cols_hbm, blocks_hbm, x_hbm, y_hbm, ritz_hbm,
    right, left, norm_ref,
    cols, blk, raw, wide, xt, yt, xo, yo, summed, ritz, shift_r, shift_l,
    tab, tab_s, ask_out, ask_in, ask_s, x_out, x_in, t_out, t_in, back, fixes, lastc, lastc_s,
    kept, kept_l, turned, parts,
    in_sem, blk_sem, loc_sem,
    ask_ss, ask_rs, x_ss, x_rs, t_ss, t_rs, o_ss, o_rs, n_ss, n_rs, all_x, all_z,
):
    me = lax.axis_index("rows")
    core = lax.axis_index("cols")
    half = peers // 2
    entries = rows * SLOTS
    layer, place = me // half, me % half
    near = (
        layer * half + (place + 1) % half,
        layer * half + (place + half - 1) % half,
        (me + half) % peers,
    )
    other = 1 - core
    side = (me // 16, (me // 4) % 4, me % 4)

    def peer(offset):
        at = [lax.rem(a + d, 4) for a, d in zip(side, offset)]
        return at[0] * 16 + at[1] * 4 + at[2]

    barrier = pltpu.get_barrier_semaphore()
    lines = [
        [peer(tuple(d if a == axis else 0 for a in range(3))) for d in range(1, 4)]
        for axis in range(3)
    ]
    met = list(near) + lines[0] + lines[1] + lines[2]
    pl.semaphore_signal(barrier, inc=1, device_id=(me, other), device_id_type=MESH)
    for to in met:
        pl.semaphore_signal(barrier, inc=1, device_id=(to, core), device_id_type=MESH)

    ins = [
        pltpu.make_async_copy(cols_hbm, cols, in_sem.at[0]),
        pltpu.make_async_copy(y_hbm, raw.at[0], in_sem.at[1]),
        pltpu.make_async_copy(x_hbm, raw.at[1], in_sem.at[2]),
        pltpu.make_async_copy(ritz_hbm, ritz, in_sem.at[3]),
    ]
    for copy in ins:
        copy.start()
    per_chunk = entries // CHUNKS

    def chunk_copy(c):
        span = pl.ds(c * per_chunk, per_chunk)
        return pltpu.make_async_copy(blocks_hbm.at[span], blk.at[span], blk_sem.at[c])

    def start_chunk(c, _):
        chunk_copy(c).start()
        return 0

    lax.fori_loop(0, CHUNKS, start_chunk, 0)

    ins[0].wait()
    col = cols[...]
    owner = col >> 6
    local = col & 63
    row_id = lax.broadcasted_iota(I32, (SLOTS, rows), 1)
    slot_id = lax.broadcasted_iota(I32, (SLOTS, rows), 0)
    order = row_id * SLOTS + slot_id

    def all_min(v):
        return jnp.min(jnp.min(v, axis=1, keepdims=True), axis=0, keepdims=True)

    def all_max(v):
        return jnp.max(jnp.max(v, axis=1, keepdims=True), axis=0, keepdims=True)

    def put(row, value):
        tab[row: row + 1, :] = jnp.broadcast_to(value, (1, 128))

    lane = lax.broadcasted_iota(I32, (1, 128), 1)
    tab[ROW_EXT: ROW_EXT + SLOTS, :rows] = jnp.where(owner == me, local, rows)
    fix = jnp.full((1, 128), 6, I32)
    pick_rows = []
    for n in range(3):
        here = owner == near[n]
        first = all_min(jnp.where(here, order, entries))
        final = all_max(jnp.where(here, order, 0))
        picks = (first, final)
        for t in range(2):
            hit = order == picks[t]
            ask_out[n, t: t + 1, :] = jnp.broadcast_to(
                all_max(jnp.where(hit, local, 0)), (1, 128)
            )
            put(ROW_PICK + 2 * n + t, jnp.minimum(picks[t], entries - 1))
            at = all_max(jnp.where(hit, row_id, 0))
            put(ROW_AT + 2 * n + t, at)
            if t == 1:
                at = jnp.where(first == final, -1, at)
            same = jnp.full((1, 1), 6, I32)
            for v, earlier in enumerate(pick_rows):
                same = jnp.where(earlier == at, v, same)
            put(ROW_SAME + 2 * n + t, same)
            fix = jnp.where(lane == at, 2 * n + t, fix)
            pick_rows.append(at)
        ask_out[n, 2:8, :] = jnp.zeros((6, 128), I32)
        put(ROW_TWO + n, (first != final).astype(I32))
    put(ROW_FIX, fix)

    asks = [
        pltpu.make_async_remote_copy(
            src_ref=ask_out.at[n], dst_ref=ask_in.at[BACK[n]],
            send_sem=ask_ss.at[n], recv_sem=ask_rs.at[BACK[n]],
            device_id=(near[n], core), device_id_type=MESH,
        )
        for n in range(3)
    ]

    col_t = jnp.transpose(
        jnp.concatenate([col.astype(F32), jnp.full((1, rows), -1.0, F32)], axis=0)
    ).astype(I32)
    src_row = lax.broadcasted_iota(I32, (rows, rows), 0)
    dst_row = lax.broadcasted_iota(I32, (rows, rows), 1)
    before, upto = src_row < dst_row, src_row <= dst_row
    src_order = src_row * SLOTS
    src_col = [jnp.broadcast_to(col_t[:, s:s + 1], (rows, rows)) for s in range(SLOTS)]
    for s in range(SLOTS):
        mine = jnp.broadcast_to(col[s:s + 1, :], (rows, rows))
        best = jnp.full((rows, rows), -1, I32)
        for t in range(SLOTS):
            best = jnp.where(
                (src_col[t] == mine) & (upto if t < s else before), src_order + t, best
            )
        found = jnp.max(best, axis=0, keepdims=True)
        found = jnp.where((found < 0) | (owner[s:s + 1, :] != me), entries, found)
        tab[ROW_PREV + s: ROW_PREV + s + 1, :rows] = found
    best = jnp.full((rows, rows), 0, I32)
    for t in range(SLOTS):
        best = jnp.where(src_col[t] == dst_row + me * rows, src_order + t, best)
    tab[ROW_LAST: ROW_LAST + 1, :rows] = jnp.max(best, axis=0, keepdims=True)
    tab_copy = pltpu.make_async_copy(tab, tab_s, loc_sem.at[0])
    tab_copy.start()

    def by_rows(index, dst):
        def widen(k, _):
            wide[pl.ds(k * rows, rows), :] = raw[index, k].astype(F32)
            return 0

        lax.fori_loop(0, vecs, widen, 0, unroll=4)

        def turn(r, _):
            dst[r] = wide[pl.ds(r, vecs, stride=rows), :].astype(BF16)
            return 0

        lax.fori_loop(0, rows, turn, 0, unroll=8)

    def across(src, dst, slot):
        return pltpu.make_async_remote_copy(
            src_ref=src, dst_ref=dst, send_sem=o_ss.at[slot], recv_sem=o_rs.at[slot],
            device_id=(me, other), device_id_type=MESH,
        )

    ins[1].wait()
    by_rows(0, yt)
    y_send = across(yt, yo, 0)
    ins[2].wait()
    by_rows(1, xt)
    x_send = across(xt.at[pl.ds(0, rows)], xo, 1)
    pl.semaphore_wait(barrier, len(met) + 1)
    for copy in asks:
        copy.start()
    for to in lines[0]:
        pl.semaphore_signal(all_x, inc=1, device_id=(to, core), device_id_type=MESH)
    y_send.start()
    x_send.start()

    ins[3].wait()
    table = ritz[...].astype(F32)
    low = core == 0
    picked = jnp.where(low, table[:, :vecs], table[:, vecs:])
    picked = jnp.concatenate(
        [jnp.where(low, picked[:vecs], picked[vecs:]), jnp.where(low, picked[vecs:], picked[:vecs])],
        axis=0,
    )
    shift_r[...] = (-jnp.transpose(picked)).astype(BF16)
    picked = jnp.where(low, table[:vecs], table[vecs:])
    picked = jnp.concatenate(
        [
            jnp.where(low, picked[:, :vecs], picked[:, vecs:]),
            jnp.where(low, picked[:, vecs:], picked[:, :vecs]),
        ],
        axis=1,
    )
    shift_l[...] = (-picked).astype(BF16)
    summed[entries] = jnp.zeros((vecs, 128), F32)

    x_backs = [
        pltpu.make_async_remote_copy(
            src_ref=x_out.at[n], dst_ref=x_in.at[BACK[n]],
            send_sem=x_ss.at[n], recv_sem=x_rs.at[BACK[n]],
            device_id=(near[n], core), device_id_type=MESH,
        )
        for n in range(3)
    ]

    xt[rows] = jnp.zeros((vecs, 128), BF16)
    tab_copy.wait()

    per_pass = rows // 4

    ask_copy = pltpu.make_async_copy(ask_in, ask_s, loc_sem.at[1])
    lastc_copy = pltpu.make_async_copy(lastc, lastc_s, loc_sem.at[2])
    t_sends = [
        pltpu.make_async_remote_copy(
            src_ref=t_out.at[n], dst_ref=t_in.at[BACK[n]],
            send_sem=t_ss.at[n], recv_sem=t_rs.at[BACK[n]],
            device_id=(near[n], core), device_id_type=MESH,
        )
        for n in range(3)
    ]

    def one_pass(c, _):
        @pl.when(c < 3)
        def _():
            chunk_copy(2 * c).wait()
            chunk_copy(2 * c + 1).wait()

        @pl.when(c == 3)
        def _():
            for last in range(6, CHUNKS):
                chunk_copy(last).wait()
            for n in range(3):
                two = jnp.broadcast_to(tab[ROW_TWO + n: ROW_TWO + n + 1, :], (vecs, 128)) > 0
                sums = [
                    jnp.dot(
                        yt[tab_s[ROW_AT + 2 * n + t, 0]], blk[tab_s[ROW_PICK + 2 * n + t, 0]],
                        preferred_element_type=F32,
                    )
                    for t in range(2)
                ]
                t_out[n, 0] = sums[0].astype(BF16)
                t_out[n, 1] = jnp.where(two, sums[1], 0.0).astype(BF16)
            for n in range(3):
                t_sends[n].start()
            for n in range(3):
                asks[n].wait()
            for n in range(3):
                for t in range(2):
                    x_out[n, t] = xt[ask_in[n, t, 0]]
                x_backs[n].start()
            ask_copy.start()
            latest = jnp.full((1, 128), 6, I32)
            for u in range(6):
                latest = jnp.where(ask_in[u // 2, u % 2: u % 2 + 1, :] == lane, u, latest)
            lastc[0:1, :] = latest
            lastc_copy.start()
            pl.semaphore_wait(all_x, 3)
            for to in lines[1]:
                pl.semaphore_signal(all_z, inc=1, device_id=(to, core), device_id_type=MESH)

        def both(i, _):
            r = c * per_pass + i
            use = [blk[r * SLOTS + s] for s in range(SLOTS)]
            prod = jnp.dot(yt[r], jnp.concatenate(use, axis=1), preferred_element_type=F32)
            lhs = [xt[tab_s[ROW_EXT + s, r]] for s in range(SLOTS)]
            kept[r] = jnp.dot(
                jnp.concatenate(lhs, axis=1),
                jnp.concatenate([block.T for block in use], axis=0),
                preferred_element_type=F32,
            )
            for s in range(SLOTS):
                summed[r * SLOTS + s] = (
                    prod[:, s * 128:(s + 1) * 128] + summed[tab_s[ROW_PREV + s, r]]
                )
            return 0

        lax.fori_loop(0, per_pass, both, 0, unroll=True)
        return 0

    lax.fori_loop(0, 4, one_pass, 0)

    x_send.wait()
    y_send.wait()

    lastc_copy.wait()
    ask_copy.wait()

    def shifts(r, totals):
        res = kept[r] + jnp.dot(
            shift_r[...], jnp.concatenate([xt[r], xo[r]], axis=0), preferred_element_type=F32
        )
        kept[r] = res
        res_l = summed[tab_s[ROW_LAST, r]] + jnp.dot(
            shift_l[...], jnp.concatenate([yt[r], yo[r]], axis=0), preferred_element_type=F32
        )
        kept_l[r] = res_l
        return (
            totals[0] + jnp.where(tab_s[ROW_FIX, r] == 6, res * res, 0.0),
            totals[1] + jnp.where(lastc_s[0, r] == 6, res_l * res_l, 0.0),
        )

    zero = jnp.zeros((vecs, 128), F32)
    right_sq, left_sq = lax.fori_loop(0, rows, shifts, (zero, zero), unroll=16)
    for u in range(6):
        turned[u] = blk[tab_s[ROW_PICK + u, 0]].T

    back[6] = zero
    for n in range(3):
        t_sends[n].wait()
    for u in range(6):
        prev = jnp.int32(6)
        for v in range(u):
            prev = jnp.where(
                ask_s[v // 2, v % 2, 0] == ask_s[u // 2, u % 2, 0], jnp.int32(v), prev
            )
        back[u] = t_in[u // 2, u % 2].astype(F32) + back[prev]
        at = ask_s[u // 2, u % 2, 0]
        res = kept_l[at] + back[u]
        left_sq += jnp.where(lastc_s[0, at] == u, res * res, 0.0)

    for n in range(3):
        x_backs[n].wait()
    fixes[6] = zero
    for u in range(6):
        fix = fixes[tab_s[ROW_SAME + u, 0]] + jnp.dot(
            x_in[u // 2, u % 2], turned[u], preferred_element_type=F32
        )
        fixes[u] = fix
        at = tab_s[ROW_AT + u, 0]
        res = kept[at] + fix
        right_sq += jnp.where(tab_s[ROW_FIX, at] == u, res * res, 0.0)

    mine = jnp.concatenate([right_sq, left_sq], axis=0)
    mine = jnp.sum(jnp.transpose(mine), axis=0, keepdims=True)
    mine = jnp.concatenate([mine, jnp.zeros((1, 128 - 2 * vecs), F32)], axis=1)
    parts[me] = mine

    def share(to):
        return pltpu.make_async_remote_copy(
            src_ref=parts.at[me], dst_ref=parts.at[me], send_sem=n_ss.at[0], recv_sem=n_rs.at[0],
            device_id=(to, core), device_id_type=MESH,
        )

    pl.semaphore_wait(all_z, 3)
    for to in ORDER[:-1]:
        share(jnp.where(me == to, ORDER[-1], to)).start()
    every = pltpu.make_async_remote_copy(
        src_ref=parts.at[pl.ds(0, peers - 1)], dst_ref=parts.at[pl.ds(0, peers - 1)],
        send_sem=n_ss.at[0], recv_sem=n_rs.at[0],
        device_id=(near[0], core), device_id_type=MESH,
    )

    def store(r, _):
        right[pl.ds(r, vecs, stride=rows), :] = kept[r] + fixes[tab_s[ROW_FIX, r]]
        left[pl.ds(r, vecs, stride=rows), :] = kept_l[r] + back[lastc_s[0, r]]
        return 0

    lax.fori_loop(0, rows, store, 0, unroll=8)
    every.wait_recv()
    every.wait_send()
    norm_ref[...] = jnp.sqrt(jnp.sum(parts[...], axis=0))


def finish(right, left, norms, right_out, left_out, right_norms, left_norms, first, second, sem):
    half = right_norms.shape[0]
    copies = [
        pltpu.make_async_copy(right, right_out, sem.at[0]),
        pltpu.make_async_copy(left, left_out, sem.at[1]),
        pltpu.make_async_copy(first, right_norms, sem.at[2]),
        pltpu.make_async_copy(second, left_norms, sem.at[3]),
    ]
    copies[0].start()
    copies[1].start()
    first[...] = norms[0, :half]
    second[...] = norms[0, half: 2 * half]
    copies[2].start()
    copies[3].start()
    for copy in copies:
        copy.wait()


def shards(blocks, col_index, right_vecs, left_vecs, ritz):
    peers = lax.axis_size("rows")
    rows, slots = col_index.shape
    vecs, _, width = right_vecs.shape
    entries = rows * slots
    any_spec = pl.BlockSpec(memory_space=pl.ANY)
    vmem = pl.BlockSpec(memory_space=pltpu.VMEM)
    dma = pltpu.SemaphoreType.DMA
    right, left, norms = pl.pallas_call(
        functools.partial(kernel, peers, rows, vecs),
        out_shape=(
            jax.ShapeDtypeStruct((vecs * rows, width), F32),
            jax.ShapeDtypeStruct((vecs * rows, width), F32),
            jax.ShapeDtypeStruct((1, 128), F32),
        ),
        in_specs=[any_spec] * 5,
        out_specs=(vmem,) * 3,
        scratch_shapes=[
            pltpu.VMEM((slots, rows), I32),
            pltpu.VMEM((entries, width, width), BF16),
            pltpu.VMEM((2, vecs, rows, width), BF16),
            pltpu.VMEM((vecs * rows, width), F32),
            pltpu.VMEM((rows + 1, vecs, width), BF16),
            pltpu.VMEM((rows, vecs, width), BF16),
            pltpu.VMEM((rows, vecs, width), BF16),
            pltpu.VMEM((rows, vecs, width), BF16),
            pltpu.VMEM((entries + 1, vecs, width), F32),
            pltpu.VMEM((2 * vecs, 2 * vecs), BF16),
            pltpu.VMEM((vecs, 2 * vecs), BF16),
            pltpu.VMEM((vecs, 2 * vecs), BF16),
            pltpu.VMEM((48, 128), I32),
            pltpu.SMEM((48, 128), I32),
            pltpu.VMEM((3, 8, 128), I32),
            pltpu.VMEM((3, 8, 128), I32),
            pltpu.SMEM((3, 8, 128), I32),
            pltpu.VMEM((3, 2, vecs, width), BF16),
            pltpu.VMEM((3, 2, vecs, width), BF16),
            pltpu.VMEM((3, 2, vecs, width), BF16),
            pltpu.VMEM((3, 2, vecs, width), BF16),
            pltpu.VMEM((7, vecs, width), F32),
            pltpu.VMEM((7, vecs, width), F32),
            pltpu.VMEM((8, 128), I32),
            pltpu.SMEM((8, 128), I32),
            pltpu.VMEM((rows, vecs, width), F32),
            pltpu.VMEM((rows, vecs, width), F32),
            pltpu.VMEM((6, width, width), BF16),
            pltpu.VMEM((peers, 1, 128), F32),
            dma((4,)),
            dma((CHUNKS,)),
            dma((3,)),
            dma((3,)), dma((3,)),
            dma((3,)), dma((3,)),
            dma((3,)), dma((3,)),
            dma((2,)), dma((2,)),
            dma((1,)), dma((1,)),
            pltpu.SemaphoreType.REGULAR, pltpu.SemaphoreType.REGULAR,
        ],
        compiler_params=pltpu.CompilerParams(
            collective_id=0, has_side_effects=True, vmem_limit_bytes=44 << 20
        ),
    )(
        *(
            pltpu.with_memory_space_constraint(arg, pltpu.HBM)
            for arg in (
                col_index.T,
                blocks.reshape(entries, width, width),
                right_vecs,
                left_vecs,
                ritz,
            )
        )
    )
    return pl.pallas_call(
        finish,
        out_shape=(
            jax.ShapeDtypeStruct((vecs, rows, width), F32),
            jax.ShapeDtypeStruct((vecs, rows, width), F32),
            jax.ShapeDtypeStruct((vecs,), F32),
            jax.ShapeDtypeStruct((vecs,), F32),
        ),
        in_specs=[vmem] * 3,
        out_specs=(any_spec,) * 4,
        scratch_shapes=[pltpu.VMEM((vecs,), F32), pltpu.VMEM((vecs,), F32), dma((4,))],
        compiler_params=pltpu.CompilerParams(vmem_limit_bytes=8 << 20),
    )(right.reshape(vecs, rows, width), left.reshape(vecs, rows, width), norms)


def solution(mesh):
    placed = (
        P("rows", None, None, None),
        P("rows", None),
        P("cols", "rows", None),
        P("cols", "rows", None),
        P(),
    )
    return jax.shard_map(
        shards,
        mesh=mesh,
        in_specs=placed,
        out_specs=(P("cols", "rows", None), P("cols", "rows", None), P("cols"), P("cols")),
        check_vma=False,
    )
```

```python
import functools

import jax
import jax.numpy as jnp
from jax import lax
from jax.experimental import pallas as pl
from jax.experimental.pallas import tpu as pltpu
from jax.sharding import PartitionSpec as P

MESH = pl.DeviceIdType.MESH
F32 = jnp.float32
BF16 = jnp.bfloat16
I32 = jnp.int32
SLOTS = 7
CHUNKS = 8
ORDER = sorted(range(64), key=lambda p: (p // 16 + p // 4 % 4 + p % 4, p))
ROW_EXT, ROW_PREV, ROW_LAST, ROW_PICK, ROW_TWO, ROW_SAME, ROW_FIX, ROW_AT = 0, 8, 16, 17, 24, 32, 38, 40
BACK = (1, 0, 2)


def kernel(
    peers, rows, vecs,
    cols_hbm, blocks_hbm, x_hbm, y_hbm, ritz_hbm,
    right, left, norm_ref,
    cols, blk, raw, wide, xt, yt, xo, yo, summed, ritz, shift_r, shift_l,
    tab, tab_s, ask_out, ask_in, ask_s, x_out, x_in, t_out, t_in, back, fixes, lastc, lastc_s,
    kept, kept_l, turned, parts,
    in_sem, blk_sem, loc_sem,
    ask_ss, ask_rs, x_ss, x_rs, t_ss, t_rs, o_ss, o_rs, n_ss, n_rs, all_x, all_z,
):
    me = lax.axis_index("rows")
    core = lax.axis_index("cols")
    half = peers // 2
    entries = rows * SLOTS
    layer, place = me // half, me % half
    near = (
        layer * half + (place + 1) % half,
        layer * half + (place + half - 1) % half,
        (me + half) % peers,
    )
    other = 1 - core
    side = (me // 16, (me // 4) % 4, me % 4)

    def peer(offset):
        at = [lax.rem(a + d, 4) for a, d in zip(side, offset)]
        return at[0] * 16 + at[1] * 4 + at[2]

    barrier = pltpu.get_barrier_semaphore()
    lines = [
        [peer(tuple(d if a == axis else 0 for a in range(3))) for d in range(1, 4)]
        for axis in range(3)
    ]
    met = list(near) + lines[0] + lines[1] + lines[2]
    pl.semaphore_signal(barrier, inc=1, device_id=(me, other), device_id_type=MESH)
    for to in met:
        pl.semaphore_signal(barrier, inc=1, device_id=(to, core), device_id_type=MESH)

    ins = [
        pltpu.make_async_copy(cols_hbm, cols, in_sem.at[0]),
        pltpu.make_async_copy(y_hbm, raw.at[0], in_sem.at[1]),
        pltpu.make_async_copy(x_hbm, raw.at[1], in_sem.at[2]),
        pltpu.make_async_copy(ritz_hbm, ritz, in_sem.at[3]),
    ]
    for copy in ins:
        copy.start()
    per_chunk = entries // CHUNKS

    def chunk_copy(c):
        span = pl.ds(c * per_chunk, per_chunk)
        return pltpu.make_async_copy(blocks_hbm.at[span], blk.at[span], blk_sem.at[c])

    def start_chunk(c, _):
        chunk_copy(c).start()
        return 0

    lax.fori_loop(0, CHUNKS, start_chunk, 0)

    ins[0].wait()
    col = cols[...]
    owner = col >> 6
    local = col & 63
    row_id = lax.broadcasted_iota(I32, (SLOTS, rows), 1)
    slot_id = lax.broadcasted_iota(I32, (SLOTS, rows), 0)
    order = row_id * SLOTS + slot_id

    def all_min(v):
        return jnp.min(jnp.min(v, axis=1, keepdims=True), axis=0, keepdims=True)

    def all_max(v):
        return jnp.max(jnp.max(v, axis=1, keepdims=True), axis=0, keepdims=True)

    def put(row, value):
        tab[row: row + 1, :] = jnp.broadcast_to(value, (1, 128))

    lane = lax.broadcasted_iota(I32, (1, 128), 1)
    tab[ROW_EXT: ROW_EXT + SLOTS, :rows] = jnp.where(owner == me, local, rows)
    fix = jnp.full((1, 128), 6, I32)
    pick_rows = []
    for n in range(3):
        here = owner == near[n]
        first = all_min(jnp.where(here, order, entries))
        final = all_max(jnp.where(here, order, 0))
        picks = (first, final)
        for t in range(2):
            hit = order == picks[t]
            ask_out[n, t: t + 1, :] = jnp.broadcast_to(
                all_max(jnp.where(hit, local, 0)), (1, 128)
            )
            put(ROW_PICK + 2 * n + t, jnp.minimum(picks[t], entries - 1))
            at = all_max(jnp.where(hit, row_id, 0))
            put(ROW_AT + 2 * n + t, at)
            if t == 1:
                at = jnp.where(first == final, -1, at)
            same = jnp.full((1, 1), 6, I32)
            for v, earlier in enumerate(pick_rows):
                same = jnp.where(earlier == at, v, same)
            put(ROW_SAME + 2 * n + t, same)
            fix = jnp.where(lane == at, 2 * n + t, fix)
            pick_rows.append(at)
        ask_out[n, 2:8, :] = jnp.zeros((6, 128), I32)
        put(ROW_TWO + n, (first != final).astype(I32))
    put(ROW_FIX, fix)

    asks = [
        pltpu.make_async_remote_copy(
            src_ref=ask_out.at[n], dst_ref=ask_in.at[BACK[n]],
            send_sem=ask_ss.at[n], recv_sem=ask_rs.at[BACK[n]],
            device_id=(near[n], core), device_id_type=MESH,
        )
        for n in range(3)
    ]

    col_t = jnp.transpose(
        jnp.concatenate([col.astype(F32), jnp.full((1, rows), -1.0, F32)], axis=0)
    ).astype(I32)
    src_row = lax.broadcasted_iota(I32, (rows, rows), 0)
    dst_row = lax.broadcasted_iota(I32, (rows, rows), 1)
    before, upto = src_row < dst_row, src_row <= dst_row
    src_order = src_row * SLOTS
    src_col = [jnp.broadcast_to(col_t[:, s:s + 1], (rows, rows)) for s in range(SLOTS)]
    for s in range(SLOTS):
        mine = jnp.broadcast_to(col[s:s + 1, :], (rows, rows))
        best = jnp.full((rows, rows), -1, I32)
        for t in range(SLOTS):
            best = jnp.where(
                (src_col[t] == mine) & (upto if t < s else before), src_order + t, best
            )
        found = jnp.max(best, axis=0, keepdims=True)
        found = jnp.where((found < 0) | (owner[s:s + 1, :] != me), entries, found)
        tab[ROW_PREV + s: ROW_PREV + s + 1, :rows] = found
    best = jnp.full((rows, rows), 0, I32)
    for t in range(SLOTS):
        best = jnp.where(src_col[t] == dst_row + me * rows, src_order + t, best)
    tab[ROW_LAST: ROW_LAST + 1, :rows] = jnp.max(best, axis=0, keepdims=True)
    tab_copy = pltpu.make_async_copy(tab, tab_s, loc_sem.at[0])
    tab_copy.start()

    def by_rows(index, dst):
        def widen(k, _):
            wide[pl.ds(k * rows, rows), :] = raw[index, k].astype(F32)
            return 0

        lax.fori_loop(0, vecs, widen, 0, unroll=4)

        def turn(r, _):
            dst[r] = wide[pl.ds(r, vecs, stride=rows), :].astype(BF16)
            return 0

        lax.fori_loop(0, rows, turn, 0, unroll=8)

    def across(src, dst, slot):
        return pltpu.make_async_remote_copy(
            src_ref=src, dst_ref=dst, send_sem=o_ss.at[slot], recv_sem=o_rs.at[slot],
            device_id=(me, other), device_id_type=MESH,
        )

    ins[1].wait()
    by_rows(0, yt)
    y_send = across(yt, yo, 0)
    ins[2].wait()
    by_rows(1, xt)
    x_send = across(xt.at[pl.ds(0, rows)], xo, 1)
    pl.semaphore_wait(barrier, len(met) + 1)
    for copy in asks:
        copy.start()
    for to in lines[0]:
        pl.semaphore_signal(all_x, inc=1, device_id=(to, core), device_id_type=MESH)
    y_send.start()
    x_send.start()

    ins[3].wait()
    table = ritz[...].astype(F32)
    low = core == 0
    picked = jnp.where(low, table[:, :vecs], table[:, vecs:])
    picked = jnp.concatenate(
        [jnp.where(low, picked[:vecs], picked[vecs:]), jnp.where(low, picked[vecs:], picked[:vecs])],
        axis=0,
    )
    shift_r[...] = (-jnp.transpose(picked)).astype(BF16)
    picked = jnp.where(low, table[:vecs], table[vecs:])
    picked = jnp.concatenate(
        [
            jnp.where(low, picked[:, :vecs], picked[:, vecs:]),
            jnp.where(low, picked[:, vecs:], picked[:, :vecs]),
        ],
        axis=1,
    )
    shift_l[...] = (-picked).astype(BF16)
    summed[entries] = jnp.zeros((vecs, 128), F32)

    x_backs = [
        pltpu.make_async_remote_copy(
            src_ref=x_out.at[n], dst_ref=x_in.at[BACK[n]],
            send_sem=x_ss.at[n], recv_sem=x_rs.at[BACK[n]],
            device_id=(near[n], core), device_id_type=MESH,
        )
        for n in range(3)
    ]

    xt[rows] = jnp.zeros((vecs, 128), BF16)
    tab_copy.wait()

    per_pass = rows // 4

    ask_copy = pltpu.make_async_copy(ask_in, ask_s, loc_sem.at[1])
    lastc_copy = pltpu.make_async_copy(lastc, lastc_s, loc_sem.at[2])
    t_sends = [
        pltpu.make_async_remote_copy(
            src_ref=t_out.at[n], dst_ref=t_in.at[BACK[n]],
            send_sem=t_ss.at[n], recv_sem=t_rs.at[BACK[n]],
            device_id=(near[n], core), device_id_type=MESH,
        )
        for n in range(3)
    ]

    def one_pass(c, _):
        @pl.when(c < 2)
        def _():
            chunk_copy(2 * c).wait()
            chunk_copy(2 * c + 1).wait()

        @pl.when(c == 2)
        def _():
            for last in range(4, CHUNKS):
                chunk_copy(last).wait()
            for n in range(3):
                two = jnp.broadcast_to(tab[ROW_TWO + n: ROW_TWO + n + 1, :], (vecs, 128)) > 0
                sums = [
                    jnp.dot(
                        yt[tab_s[ROW_AT + 2 * n + t, 0]], blk[tab_s[ROW_PICK + 2 * n + t, 0]],
                        preferred_element_type=F32,
                    )
                    for t in range(2)
                ]
                t_out[n, 0] = sums[0].astype(BF16)
                t_out[n, 1] = jnp.where(two, sums[1], 0.0).astype(BF16)
            for n in range(3):
                t_sends[n].start()
        @pl.when(c == 3)
        def _():
            for n in (2, 0, 1):
                asks[BACK[n]].wait()
                for t in range(2):
                    x_out[n, t] = xt[ask_in[n, t, 0]]
                x_backs[n].start()
            ask_copy.start()
            latest = jnp.full((1, 128), 6, I32)
            for u in range(6):
                latest = jnp.where(ask_in[u // 2, u % 2: u % 2 + 1, :] == lane, u, latest)
            lastc[0:1, :] = latest
            lastc_copy.start()
            pl.semaphore_wait(all_x, 3)
            for to in lines[1]:
                pl.semaphore_signal(all_z, inc=1, device_id=(to, core), device_id_type=MESH)

        def both(i, _):
            r = c * per_pass + i
            use = [blk[r * SLOTS + s] for s in range(SLOTS)]
            prod = jnp.dot(yt[r], jnp.concatenate(use, axis=1), preferred_element_type=F32)
            lhs = [xt[tab_s[ROW_EXT + s, r]] for s in range(SLOTS)]
            kept[r] = jnp.dot(
                jnp.concatenate(lhs, axis=1),
                jnp.concatenate([block.T for block in use], axis=0),
                preferred_element_type=F32,
            )
            for s in range(SLOTS):
                summed[r * SLOTS + s] = (
                    prod[:, s * 128:(s + 1) * 128] + summed[tab_s[ROW_PREV + s, r]]
                )
            return 0

        lax.fori_loop(0, per_pass, both, 0, unroll=True)
        return 0

    lax.fori_loop(0, 4, one_pass, 0)

    x_send.wait()
    y_send.wait()

    lastc_copy.wait()
    ask_copy.wait()

    def shifts(r, totals):
        res = kept[r] + jnp.dot(
            shift_r[...], jnp.concatenate([xt[r], xo[r]], axis=0), preferred_element_type=F32
        )
        kept[r] = res
        res_l = summed[tab_s[ROW_LAST, r]] + jnp.dot(
            shift_l[...], jnp.concatenate([yt[r], yo[r]], axis=0), preferred_element_type=F32
        )
        kept_l[r] = res_l
        return (
            totals[0] + jnp.where(tab_s[ROW_FIX, r] == 6, res * res, 0.0),
            totals[1] + jnp.where(lastc_s[0, r] == 6, res_l * res_l, 0.0),
        )

    zero = jnp.zeros((vecs, 128), F32)
    right_sq, left_sq = lax.fori_loop(0, rows, shifts, (zero, zero), unroll=16)
    for u in range(6):
        turned[u] = blk[tab_s[ROW_PICK + u, 0]].T

    back[6] = zero
    for n in range(3):
        t_sends[n].wait()
    for u in range(6):
        prev = jnp.int32(6)
        for v in range(u):
            prev = jnp.where(
                ask_s[v // 2, v % 2, 0] == ask_s[u // 2, u % 2, 0], jnp.int32(v), prev
            )
        back[u] = t_in[u // 2, u % 2].astype(F32) + back[prev]
        at = ask_s[u // 2, u % 2, 0]
        res = kept_l[at] + back[u]
        left_sq += jnp.where(lastc_s[0, at] == u, res * res, 0.0)

    for n in range(3):
        x_backs[n].wait()
    fixes[6] = zero
    for u in range(6):
        fix = fixes[tab_s[ROW_SAME + u, 0]] + jnp.dot(
            x_in[u // 2, u % 2], turned[u], preferred_element_type=F32
        )
        fixes[u] = fix
        at = tab_s[ROW_AT + u, 0]
        res = kept[at] + fix
        right_sq += jnp.where(tab_s[ROW_FIX, at] == u, res * res, 0.0)

    mine = jnp.concatenate([right_sq, left_sq], axis=0)
    mine = jnp.sum(jnp.transpose(mine), axis=0, keepdims=True)
    mine = jnp.concatenate([mine, jnp.zeros((1, 128 - 2 * vecs), F32)], axis=1)
    parts[me] = mine

    def share(to):
        return pltpu.make_async_remote_copy(
            src_ref=parts.at[me], dst_ref=parts.at[me], send_sem=n_ss.at[0], recv_sem=n_rs.at[0],
            device_id=(to, core), device_id_type=MESH,
        )

    pl.semaphore_wait(all_z, 3)
    for to in ORDER[:-1]:
        share(jnp.where(me == to, ORDER[-1], to)).start()
    every = pltpu.make_async_remote_copy(
        src_ref=parts.at[pl.ds(0, peers - 1)], dst_ref=parts.at[pl.ds(0, peers - 1)],
        send_sem=n_ss.at[0], recv_sem=n_rs.at[0],
        device_id=(near[0], core), device_id_type=MESH,
    )

    def store(r, _):
        right[pl.ds(r, vecs, stride=rows), :] = kept[r] + fixes[tab_s[ROW_FIX, r]]
        left[pl.ds(r, vecs, stride=rows), :] = kept_l[r] + back[lastc_s[0, r]]
        return 0

    lax.fori_loop(0, rows, store, 0, unroll=8)
    every.wait_recv()
    every.wait_send()
    norm_ref[...] = jnp.sqrt(jnp.sum(parts[...], axis=0))


def finish(right, left, norms, right_out, left_out, right_norms, left_norms, first, second, sem):
    half = right_norms.shape[0]
    copies = [
        pltpu.make_async_copy(right, right_out, sem.at[0]),
        pltpu.make_async_copy(left, left_out, sem.at[1]),
        pltpu.make_async_copy(first, right_norms, sem.at[2]),
        pltpu.make_async_copy(second, left_norms, sem.at[3]),
    ]
    copies[0].start()
    copies[1].start()
    first[...] = norms[0, :half]
    second[...] = norms[0, half: 2 * half]
    copies[2].start()
    copies[3].start()
    for copy in copies:
        copy.wait()


def shards(blocks, col_index, right_vecs, left_vecs, ritz):
    peers = lax.axis_size("rows")
    rows, slots = col_index.shape
    vecs, _, width = right_vecs.shape
    entries = rows * slots
    any_spec = pl.BlockSpec(memory_space=pl.ANY)
    vmem = pl.BlockSpec(memory_space=pltpu.VMEM)
    dma = pltpu.SemaphoreType.DMA
    right, left, norms = pl.pallas_call(
        functools.partial(kernel, peers, rows, vecs),
        out_shape=(
            jax.ShapeDtypeStruct((vecs * rows, width), F32),
            jax.ShapeDtypeStruct((vecs * rows, width), F32),
            jax.ShapeDtypeStruct((1, 128), F32),
        ),
        in_specs=[any_spec] * 5,
        out_specs=(vmem,) * 3,
        scratch_shapes=[
            pltpu.VMEM((slots, rows), I32),
            pltpu.VMEM((entries, width, width), BF16),
            pltpu.VMEM((2, vecs, rows, width), BF16),
            pltpu.VMEM((vecs * rows, width), F32),
            pltpu.VMEM((rows + 1, vecs, width), BF16),
            pltpu.VMEM((rows, vecs, width), BF16),
            pltpu.VMEM((rows, vecs, width), BF16),
            pltpu.VMEM((rows, vecs, width), BF16),
            pltpu.VMEM((entries + 1, vecs, width), F32),
            pltpu.VMEM((2 * vecs, 2 * vecs), BF16),
            pltpu.VMEM((vecs, 2 * vecs), BF16),
            pltpu.VMEM((vecs, 2 * vecs), BF16),
            pltpu.VMEM((48, 128), I32),
            pltpu.SMEM((48, 128), I32),
            pltpu.VMEM((3, 8, 128), I32),
            pltpu.VMEM((3, 8, 128), I32),
            pltpu.SMEM((3, 8, 128), I32),
            pltpu.VMEM((3, 2, vecs, width), BF16),
            pltpu.VMEM((3, 2, vecs, width), BF16),
            pltpu.VMEM((3, 2, vecs, width), BF16),
            pltpu.VMEM((3, 2, vecs, width), BF16),
            pltpu.VMEM((7, vecs, width), F32),
            pltpu.VMEM((7, vecs, width), F32),
            pltpu.VMEM((8, 128), I32),
            pltpu.SMEM((8, 128), I32),
            pltpu.VMEM((rows, vecs, width), F32),
            pltpu.VMEM((rows, vecs, width), F32),
            pltpu.VMEM((6, width, width), BF16),
            pltpu.VMEM((peers, 1, 128), F32),
            dma((4,)),
            dma((CHUNKS,)),
            dma((3,)),
            dma((3,)), dma((3,)),
            dma((3,)), dma((3,)),
            dma((3,)), dma((3,)),
            dma((2,)), dma((2,)),
            dma((1,)), dma((1,)),
            pltpu.SemaphoreType.REGULAR, pltpu.SemaphoreType.REGULAR,
        ],
        compiler_params=pltpu.CompilerParams(
            collective_id=0, has_side_effects=True, vmem_limit_bytes=44 << 20
        ),
    )(
        *(
            pltpu.with_memory_space_constraint(arg, pltpu.HBM)
            for arg in (
                col_index.T,
                blocks.reshape(entries, width, width),
                right_vecs,
                left_vecs,
                ritz,
            )
        )
    )
    return pl.pallas_call(
        finish,
        out_shape=(
            jax.ShapeDtypeStruct((vecs, rows, width), F32),
            jax.ShapeDtypeStruct((vecs, rows, width), F32),
            jax.ShapeDtypeStruct((vecs,), F32),
            jax.ShapeDtypeStruct((vecs,), F32),
        ),
        in_specs=[vmem] * 3,
        out_specs=(any_spec,) * 4,
        scratch_shapes=[pltpu.VMEM((vecs,), F32), pltpu.VMEM((vecs,), F32), dma((4,))],
        compiler_params=pltpu.CompilerParams(vmem_limit_bytes=8 << 20),
    )(right.reshape(vecs, rows, width), left.reshape(vecs, rows, width), norms)


def solution(mesh):
    placed = (
        P("rows", None, None, None),
        P("rows", None),
        P("cols", "rows", None),
        P("cols", "rows", None),
        P(),
    )
    return jax.shard_map(
        shards,
        mesh=mesh,
        in_specs=placed,
        out_specs=(P("cols", "rows", None), P("cols", "rows", None), P("cols"), P("cols")),
        check_vma=False,
    )
```

```python
import functools

import jax
import jax.numpy as jnp
from jax import lax
from jax.experimental import pallas as pl
from jax.experimental.pallas import tpu as pltpu
from jax.sharding import PartitionSpec as P

MESH = pl.DeviceIdType.MESH
F32 = jnp.float32
BF16 = jnp.bfloat16
I32 = jnp.int32
SLOTS = 7
CHUNKS = 8
ORDER = sorted(range(64), key=lambda p: (p // 16 + p // 4 % 4 + p % 4, p))
ROW_EXT, ROW_PREV, ROW_LAST, ROW_PICK, ROW_TWO, ROW_SAME, ROW_FIX, ROW_AT = 0, 8, 16, 17, 24, 32, 38, 40
BACK = (1, 0, 2)


def kernel(
    peers, rows, vecs,
    cols_hbm, blocks_hbm, x_hbm, y_hbm, ritz_hbm,
    right, left, norm_ref,
    cols, blk, raw, wide, xt, yt, xo, yo, summed, ritz, shift_r, shift_l,
    tab, tab_s, ask_out, ask_in, ask_s, x_out, x_in, t_out, t_in, back, fixes, lastc, lastc_s,
    kept, kept_l, turned, parts,
    in_sem, blk_sem, loc_sem,
    ask_ss, ask_rs, x_ss, x_rs, t_ss, t_rs, o_ss, o_rs, n_ss, n_rs, all_x, all_z,
):
    me = lax.axis_index("rows")
    core = lax.axis_index("cols")
    half = peers // 2
    entries = rows * SLOTS
    layer, place = me // half, me % half
    near = (
        layer * half + (place + 1) % half,
        layer * half + (place + half - 1) % half,
        (me + half) % peers,
    )
    other = 1 - core
    side = (me // 16, (me // 4) % 4, me % 4)

    def peer(offset):
        at = [lax.rem(a + d, 4) for a, d in zip(side, offset)]
        return at[0] * 16 + at[1] * 4 + at[2]

    barrier = pltpu.get_barrier_semaphore()
    lines = [
        [peer(tuple(d if a == axis else 0 for a in range(3))) for d in range(1, 4)]
        for axis in range(3)
    ]
    met = list(near) + lines[0] + lines[1] + lines[2]
    pl.semaphore_signal(barrier, inc=1, device_id=(me, other), device_id_type=MESH)
    for to in met:
        pl.semaphore_signal(barrier, inc=1, device_id=(to, core), device_id_type=MESH)

    ins = [
        pltpu.make_async_copy(cols_hbm, cols, in_sem.at[0]),
        pltpu.make_async_copy(y_hbm, raw.at[0], in_sem.at[1]),
        pltpu.make_async_copy(x_hbm, raw.at[1], in_sem.at[2]),
        pltpu.make_async_copy(ritz_hbm, ritz, in_sem.at[3]),
    ]
    for copy in ins:
        copy.start()
    per_chunk = entries // CHUNKS

    def chunk_copy(c):
        span = pl.ds(c * per_chunk, per_chunk)
        return pltpu.make_async_copy(blocks_hbm.at[span], blk.at[span], blk_sem.at[c])

    def start_chunk(c, _):
        chunk_copy(c).start()
        return 0

    lax.fori_loop(0, CHUNKS // 2, start_chunk, 0)

    ins[0].wait()
    col = cols[...]
    owner = col >> 6
    local = col & 63
    row_id = lax.broadcasted_iota(I32, (SLOTS, rows), 1)
    slot_id = lax.broadcasted_iota(I32, (SLOTS, rows), 0)
    order = row_id * SLOTS + slot_id

    def all_min(v):
        return jnp.min(jnp.min(v, axis=1, keepdims=True), axis=0, keepdims=True)

    def all_max(v):
        return jnp.max(jnp.max(v, axis=1, keepdims=True), axis=0, keepdims=True)

    def put(row, value):
        tab[row: row + 1, :] = jnp.broadcast_to(value, (1, 128))

    lane = lax.broadcasted_iota(I32, (1, 128), 1)
    tab[ROW_EXT: ROW_EXT + SLOTS, :rows] = jnp.where(owner == me, local, rows)
    fix = jnp.full((1, 128), 6, I32)
    pick_rows = []
    for n in range(3):
        here = owner == near[n]
        first = all_min(jnp.where(here, order, entries))
        final = all_max(jnp.where(here, order, 0))
        picks = (first, final)
        for t in range(2):
            hit = order == picks[t]
            ask_out[n, t: t + 1, :] = jnp.broadcast_to(
                all_max(jnp.where(hit, local, 0)), (1, 128)
            )
            put(ROW_PICK + 2 * n + t, jnp.minimum(picks[t], entries - 1))
            at = all_max(jnp.where(hit, row_id, 0))
            put(ROW_AT + 2 * n + t, at)
            if t == 1:
                at = jnp.where(first == final, -1, at)
            same = jnp.full((1, 1), 6, I32)
            for v, earlier in enumerate(pick_rows):
                same = jnp.where(earlier == at, v, same)
            put(ROW_SAME + 2 * n + t, same)
            fix = jnp.where(lane == at, 2 * n + t, fix)
            pick_rows.append(at)
        ask_out[n, 2:8, :] = jnp.zeros((6, 128), I32)
        put(ROW_TWO + n, (first != final).astype(I32))
    put(ROW_FIX, fix)

    asks = [
        pltpu.make_async_remote_copy(
            src_ref=ask_out.at[n], dst_ref=ask_in.at[BACK[n]],
            send_sem=ask_ss.at[n], recv_sem=ask_rs.at[BACK[n]],
            device_id=(near[n], core), device_id_type=MESH,
        )
        for n in range(3)
    ]

    col_t = jnp.transpose(
        jnp.concatenate([col.astype(F32), jnp.full((1, rows), -1.0, F32)], axis=0)
    ).astype(I32)
    src_row = lax.broadcasted_iota(I32, (rows, rows), 0)
    dst_row = lax.broadcasted_iota(I32, (rows, rows), 1)
    before, upto = src_row < dst_row, src_row <= dst_row
    src_order = src_row * SLOTS
    src_col = [jnp.broadcast_to(col_t[:, s:s + 1], (rows, rows)) for s in range(SLOTS)]
    for s in range(SLOTS):
        mine = jnp.broadcast_to(col[s:s + 1, :], (rows, rows))
        best = jnp.full((rows, rows), -1, I32)
        for t in range(SLOTS):
            best = jnp.where(
                (src_col[t] == mine) & (upto if t < s else before), src_order + t, best
            )
        found = jnp.max(best, axis=0, keepdims=True)
        found = jnp.where((found < 0) | (owner[s:s + 1, :] != me), entries, found)
        tab[ROW_PREV + s: ROW_PREV + s + 1, :rows] = found
    best = jnp.full((rows, rows), 0, I32)
    for t in range(SLOTS):
        best = jnp.where(src_col[t] == dst_row + me * rows, src_order + t, best)
    tab[ROW_LAST: ROW_LAST + 1, :rows] = jnp.max(best, axis=0, keepdims=True)
    tab_copy = pltpu.make_async_copy(tab, tab_s, loc_sem.at[0])
    tab_copy.start()

    def by_rows(index, dst):
        def widen(k, _):
            wide[pl.ds(k * rows, rows), :] = raw[index, k].astype(F32)
            return 0

        lax.fori_loop(0, vecs, widen, 0, unroll=4)

        def turn(r, _):
            dst[r] = wide[pl.ds(r, vecs, stride=rows), :].astype(BF16)
            return 0

        lax.fori_loop(0, rows, turn, 0, unroll=8)

    def across(src, dst, slot):
        return pltpu.make_async_remote_copy(
            src_ref=src, dst_ref=dst, send_sem=o_ss.at[slot], recv_sem=o_rs.at[slot],
            device_id=(me, other), device_id_type=MESH,
        )

    ins[1].wait()
    by_rows(0, yt)
    y_send = across(yt, yo, 0)
    ins[2].wait()
    by_rows(1, xt)
    x_send = across(xt.at[pl.ds(0, rows)], xo, 1)
    pl.semaphore_wait(barrier, len(met) + 1)
    for copy in asks:
        copy.start()
    for to in lines[0]:
        pl.semaphore_signal(all_x, inc=1, device_id=(to, core), device_id_type=MESH)
    y_send.start()
    x_send.start()

    ins[3].wait()
    table = ritz[...].astype(F32)
    low = core == 0
    picked = jnp.where(low, table[:, :vecs], table[:, vecs:])
    picked = jnp.concatenate(
        [jnp.where(low, picked[:vecs], picked[vecs:]), jnp.where(low, picked[vecs:], picked[:vecs])],
        axis=0,
    )
    shift_r[...] = (-jnp.transpose(picked)).astype(BF16)
    picked = jnp.where(low, table[:vecs], table[vecs:])
    picked = jnp.concatenate(
        [
            jnp.where(low, picked[:, :vecs], picked[:, vecs:]),
            jnp.where(low, picked[:, vecs:], picked[:, :vecs]),
        ],
        axis=1,
    )
    shift_l[...] = (-picked).astype(BF16)
    summed[entries] = jnp.zeros((vecs, 128), F32)

    x_backs = [
        pltpu.make_async_remote_copy(
            src_ref=x_out.at[n], dst_ref=x_in.at[BACK[n]],
            send_sem=x_ss.at[n], recv_sem=x_rs.at[BACK[n]],
            device_id=(near[n], core), device_id_type=MESH,
        )
        for n in range(3)
    ]

    xt[rows] = jnp.zeros((vecs, 128), BF16)
    tab_copy.wait()

    per_pass = rows // 4

    ask_copy = pltpu.make_async_copy(ask_in, ask_s, loc_sem.at[1])
    lastc_copy = pltpu.make_async_copy(lastc, lastc_s, loc_sem.at[2])
    t_sends = [
        pltpu.make_async_remote_copy(
            src_ref=t_out.at[n], dst_ref=t_in.at[BACK[n]],
            send_sem=t_ss.at[n], recv_sem=t_rs.at[BACK[n]],
            device_id=(near[n], core), device_id_type=MESH,
        )
        for n in range(3)
    ]

    def one_pass(c, _):
        @pl.when(c < 3)
        def _():
            chunk_copy(2 * c).wait()
            chunk_copy(2 * c + 1).wait()

        @pl.when(c < 2)
        def _():
            chunk_copy(2 * c + 4).start()
            chunk_copy(2 * c + 5).start()

        @pl.when(c == 3)
        def _():
            for last in range(6, CHUNKS):
                chunk_copy(last).wait()
            for n in range(3):
                two = jnp.broadcast_to(tab[ROW_TWO + n: ROW_TWO + n + 1, :], (vecs, 128)) > 0
                sums = [
                    jnp.dot(
                        yt[tab_s[ROW_AT + 2 * n + t, 0]], blk[tab_s[ROW_PICK + 2 * n + t, 0]],
                        preferred_element_type=F32,
                    )
                    for t in range(2)
                ]
                t_out[n, 0] = sums[0].astype(BF16)
                t_out[n, 1] = jnp.where(two, sums[1], 0.0).astype(BF16)
            for n in range(3):
                t_sends[n].start()
            for n in range(3):
                asks[n].wait()
            for n in range(3):
                for t in range(2):
                    x_out[n, t] = xt[ask_in[n, t, 0]]
                x_backs[n].start()
            ask_copy.start()
            latest = jnp.full((1, 128), 6, I32)
            for u in range(6):
                latest = jnp.where(ask_in[u // 2, u % 2: u % 2 + 1, :] == lane, u, latest)
            lastc[0:1, :] = latest
            lastc_copy.start()
            pl.semaphore_wait(all_x, 3)
            for to in lines[1]:
                pl.semaphore_signal(all_z, inc=1, device_id=(to, core), device_id_type=MESH)

        def both(i, _):
            r = c * per_pass + i
            use = [blk[r * SLOTS + s] for s in range(SLOTS)]
            prod = jnp.dot(yt[r], jnp.concatenate(use, axis=1), preferred_element_type=F32)
            lhs = [xt[tab_s[ROW_EXT + s, r]] for s in range(SLOTS)]
            kept[r] = jnp.dot(
                jnp.concatenate(lhs, axis=1),
                jnp.concatenate([block.T for block in use], axis=0),
                preferred_element_type=F32,
            )
            for s in range(SLOTS):
                summed[r * SLOTS + s] = (
                    prod[:, s * 128:(s + 1) * 128] + summed[tab_s[ROW_PREV + s, r]]
                )
            return 0

        lax.fori_loop(0, per_pass, both, 0, unroll=True)
        return 0

    lax.fori_loop(0, 4, one_pass, 0)

    x_send.wait()
    y_send.wait()

    lastc_copy.wait()
    ask_copy.wait()

    def shifts(r, totals):
        res = kept[r] + jnp.dot(
            shift_r[...], jnp.concatenate([xt[r], xo[r]], axis=0), preferred_element_type=F32
        )
        kept[r] = res
        res_l = summed[tab_s[ROW_LAST, r]] + jnp.dot(
            shift_l[...], jnp.concatenate([yt[r], yo[r]], axis=0), preferred_element_type=F32
        )
        kept_l[r] = res_l
        return (
            totals[0] + jnp.where(tab_s[ROW_FIX, r] == 6, res * res, 0.0),
            totals[1] + jnp.where(lastc_s[0, r] == 6, res_l * res_l, 0.0),
        )

    zero = jnp.zeros((vecs, 128), F32)
    right_sq, left_sq = lax.fori_loop(0, rows, shifts, (zero, zero), unroll=16)
    for u in range(6):
        turned[u] = blk[tab_s[ROW_PICK + u, 0]].T

    back[6] = zero
    for n in range(3):
        t_sends[n].wait()
    for u in range(6):
        prev = jnp.int32(6)
        for v in range(u):
            prev = jnp.where(
                ask_s[v // 2, v % 2, 0] == ask_s[u // 2, u % 2, 0], jnp.int32(v), prev
            )
        back[u] = t_in[u // 2, u % 2].astype(F32) + back[prev]
        at = ask_s[u // 2, u % 2, 0]
        res = kept_l[at] + back[u]
        left_sq += jnp.where(lastc_s[0, at] == u, res * res, 0.0)

    for n in range(3):
        x_backs[n].wait()
    fixes[6] = zero
    for u in range(6):
        fix = fixes[tab_s[ROW_SAME + u, 0]] + jnp.dot(
            x_in[u // 2, u % 2], turned[u], preferred_element_type=F32
        )
        fixes[u] = fix
        at = tab_s[ROW_AT + u, 0]
        res = kept[at] + fix
        right_sq += jnp.where(tab_s[ROW_FIX, at] == u, res * res, 0.0)

    mine = jnp.concatenate([right_sq, left_sq], axis=0)
    mine = jnp.sum(jnp.transpose(mine), axis=0, keepdims=True)
    mine = jnp.concatenate([mine, jnp.zeros((1, 128 - 2 * vecs), F32)], axis=1)
    parts[me] = mine

    def share(to):
        return pltpu.make_async_remote_copy(
            src_ref=parts.at[me], dst_ref=parts.at[me], send_sem=n_ss.at[0], recv_sem=n_rs.at[0],
            device_id=(to, core), device_id_type=MESH,
        )

    pl.semaphore_wait(all_z, 3)
    for to in ORDER[:-1]:
        share(jnp.where(me == to, ORDER[-1], to)).start()
    every = pltpu.make_async_remote_copy(
        src_ref=parts.at[pl.ds(0, peers - 1)], dst_ref=parts.at[pl.ds(0, peers - 1)],
        send_sem=n_ss.at[0], recv_sem=n_rs.at[0],
        device_id=(near[0], core), device_id_type=MESH,
    )

    def store(r, _):
        right[pl.ds(r, vecs, stride=rows), :] = kept[r] + fixes[tab_s[ROW_FIX, r]]
        left[pl.ds(r, vecs, stride=rows), :] = kept_l[r] + back[lastc_s[0, r]]
        return 0

    lax.fori_loop(0, rows, store, 0, unroll=8)
    every.wait_recv()
    every.wait_send()
    norm_ref[...] = jnp.sqrt(jnp.sum(parts[...], axis=0))


def finish(right, left, norms, right_out, left_out, right_norms, left_norms, first, second, sem):
    half = right_norms.shape[0]
    copies = [
        pltpu.make_async_copy(right, right_out, sem.at[0]),
        pltpu.make_async_copy(left, left_out, sem.at[1]),
        pltpu.make_async_copy(first, right_norms, sem.at[2]),
        pltpu.make_async_copy(second, left_norms, sem.at[3]),
    ]
    copies[0].start()
    copies[1].start()
    first[...] = norms[0, :half]
    second[...] = norms[0, half: 2 * half]
    copies[2].start()
    copies[3].start()
    for copy in copies:
        copy.wait()


def shards(blocks, col_index, right_vecs, left_vecs, ritz):
    peers = lax.axis_size("rows")
    rows, slots = col_index.shape
    vecs, _, width = right_vecs.shape
    entries = rows * slots
    any_spec = pl.BlockSpec(memory_space=pl.ANY)
    vmem = pl.BlockSpec(memory_space=pltpu.VMEM)
    dma = pltpu.SemaphoreType.DMA
    right, left, norms = pl.pallas_call(
        functools.partial(kernel, peers, rows, vecs),
        out_shape=(
            jax.ShapeDtypeStruct((vecs * rows, width), F32),
            jax.ShapeDtypeStruct((vecs * rows, width), F32),
            jax.ShapeDtypeStruct((1, 128), F32),
        ),
        in_specs=[any_spec] * 5,
        out_specs=(vmem,) * 3,
        scratch_shapes=[
            pltpu.VMEM((slots, rows), I32),
            pltpu.VMEM((entries, width, width), BF16),
            pltpu.VMEM((2, vecs, rows, width), BF16),
            pltpu.VMEM((vecs * rows, width), F32),
            pltpu.VMEM((rows + 1, vecs, width), BF16),
            pltpu.VMEM((rows, vecs, width), BF16),
            pltpu.VMEM((rows, vecs, width), BF16),
            pltpu.VMEM((rows, vecs, width), BF16),
            pltpu.VMEM((entries + 1, vecs, width), F32),
            pltpu.VMEM((2 * vecs, 2 * vecs), BF16),
            pltpu.VMEM((vecs, 2 * vecs), BF16),
            pltpu.VMEM((vecs, 2 * vecs), BF16),
            pltpu.VMEM((48, 128), I32),
            pltpu.SMEM((48, 128), I32),
            pltpu.VMEM((3, 8, 128), I32),
            pltpu.VMEM((3, 8, 128), I32),
            pltpu.SMEM((3, 8, 128), I32),
            pltpu.VMEM((3, 2, vecs, width), BF16),
            pltpu.VMEM((3, 2, vecs, width), BF16),
            pltpu.VMEM((3, 2, vecs, width), BF16),
            pltpu.VMEM((3, 2, vecs, width), BF16),
            pltpu.VMEM((7, vecs, width), F32),
            pltpu.VMEM((7, vecs, width), F32),
            pltpu.VMEM((8, 128), I32),
            pltpu.SMEM((8, 128), I32),
            pltpu.VMEM((rows, vecs, width), F32),
            pltpu.VMEM((rows, vecs, width), F32),
            pltpu.VMEM((6, width, width), BF16),
            pltpu.VMEM((peers, 1, 128), F32),
            dma((4,)),
            dma((CHUNKS,)),
            dma((3,)),
            dma((3,)), dma((3,)),
            dma((3,)), dma((3,)),
            dma((3,)), dma((3,)),
            dma((2,)), dma((2,)),
            dma((1,)), dma((1,)),
            pltpu.SemaphoreType.REGULAR, pltpu.SemaphoreType.REGULAR,
        ],
        compiler_params=pltpu.CompilerParams(
            collective_id=0, has_side_effects=True, vmem_limit_bytes=44 << 20
        ),
    )(
        *(
            pltpu.with_memory_space_constraint(arg, pltpu.HBM)
            for arg in (
                col_index.T,
                blocks.reshape(entries, width, width),
                right_vecs,
                left_vecs,
                ritz,
            )
        )
    )
    return pl.pallas_call(
        finish,
        out_shape=(
            jax.ShapeDtypeStruct((vecs, rows, width), F32),
            jax.ShapeDtypeStruct((vecs, rows, width), F32),
            jax.ShapeDtypeStruct((vecs,), F32),
            jax.ShapeDtypeStruct((vecs,), F32),
        ),
        in_specs=[vmem] * 3,
        out_specs=(any_spec,) * 4,
        scratch_shapes=[pltpu.VMEM((vecs,), F32), pltpu.VMEM((vecs,), F32), dma((4,))],
        compiler_params=pltpu.CompilerParams(vmem_limit_bytes=8 << 20),
    )(right.reshape(vecs, rows, width), left.reshape(vecs, rows, width), norms)


def solution(mesh):
    placed = (
        P("rows", None, None, None),
        P("rows", None),
        P("cols", "rows", None),
        P("cols", "rows", None),
        P(),
    )
    return jax.shard_map(
        shards,
        mesh=mesh,
        in_specs=placed,
        out_specs=(P("cols", "rows", None), P("cols", "rows", None), P("cols"), P("cols")),
        check_vma=False,
    )
```
